256 devices in a mesh: grp: 16 (over z, core), sp: 16 (over y, x).
Axes of the slice: x: 4, y: 4, z: 8, core: 2. Of those that a mesh axis runs over, the one named last changes fastest.
Arguments:
- queries: bfloat16 [32768, 2048], P(('grp', 'sp')), may hold values from -9 to 9
- keys: bfloat16 [32768, 512], P(('grp', 'sp')), may hold values from -9 to 9
- values: bfloat16 [32768, 512], P(('grp', 'sp')), may hold values from -6 to 6
- grad_out: bfloat16 [32768, 2048], P(('grp', 'sp')), may hold values from -6 to 6
- doc_ids: int32 [32768], P(('grp', 'sp')), may hold values from 0 to 63, never falling along the last dimension, each value on 1 to 2048 neighbouring positions
Outputs:
- grad_queries: bfloat16 [32768, 2048], P(('grp', 'sp'))
- grad_keys: bfloat16 [32768, 512], P(('grp', 'sp'))
- grad_values: bfloat16 [32768, 512], P(('grp', 'sp'))
The draws below stay inside these ranges and needn't reach their ends.
Inputs may be any that keep to these rules, and one draw needn't show every extreme that they name: `doc_ids`: document numbers never fall along the stream; every document has 1 to 2048 tokens and one has exactly 2048.
All inputs are finite; a program needn't handle non-finite values.
Results may differ from the reference program's by a relative error of at most 0.0066.
Values may be sent and summed in bfloat16 or wider, within the bound.
A program may use at most 128 MiB of HBM per device.

```python
import math
import jax
import jax.numpy as jnp
import numpy as np
from jax import lax

HEADS = 16
KV_HEADS = 4
HEAD_DIM = 128
SEQ = 2048
TOKENS = 32768
DOCS = 64


def draw_queries(key, part):
    key = jax.random.fold_in(key, 3)
    result = jnp.clip(jax.random.normal(key, (TOKENS, HEADS, HEAD_DIM), jnp.float32), -5.0, 5.0)
    return result.reshape(TOKENS, HEADS * HEAD_DIM).astype(jnp.bfloat16)


def draw_keys(key, part):
    key = jax.random.fold_in(key, 5)
    result = jnp.clip(jax.random.normal(key, (TOKENS, KV_HEADS, HEAD_DIM), jnp.float32), -5.0, 5.0)
    return result.reshape(TOKENS, KV_HEADS * HEAD_DIM).astype(jnp.bfloat16)


def level_of(rng, extent, split, least, top_value):
    factor_of, own = 1.0, jax.random.fold_in(rng, 6)
    for axis_at, blocks in split:
        heights = jnp.exp(jax.random.uniform(jax.random.fold_in(own, axis_at), (blocks,), jnp.float32, least / len(split), top_value / len(split)))
        factor_of = factor_of * jnp.repeat(heights, extent[axis_at] // blocks).reshape([-1 if axis == axis_at else 1 for axis in range(len(extent))])
    return factor_of


def length_profile(amount, total, reach, lean):
    loads = [(1 << 20) // math.isqrt(rank ** lean) + 1 for rank in range(2, amount + 1)]
    surplus, holding = total - reach - (amount - 1), [1] * (amount - 1)
    while surplus > 0:
        movable = [i for i in range(amount - 1) if holding[i] < reach]
        pool, remaining = sum([loads[i] for i in movable]), surplus
        for i in movable:
            extra = min(reach - holding[i], max(1, remaining * loads[i] // pool), surplus)
            holding[i] = holding[i] + extra
            surplus = surplus - extra
    return np.array([reach] + holding)


def uneven(stream_key, number_of, total, bound, skew):
    if number_of == 2:
        one = jax.random.randint(stream_key, (), max(1, total - bound), min(bound, total - 1) + 1)
        return jnp.stack([one, total - one])
    sizes = jnp.asarray(length_profile(number_of, total, bound, skew), jnp.int32)
    pairs = (number_of - 1) // 2
    source_of, sink = sizes[1:1 + 2 * pairs:2], sizes[2:2 + 2 * pairs:2]
    margin = jnp.minimum(source_of - 1, bound - sink)
    moved = jax.random.randint(jax.random.fold_in(stream_key, 1), (pairs,), 0, 1 << 20) % (margin + 1)
    sizes = sizes.at[1:1 + 2 * pairs:2].set(source_of - moved).at[2:2 + 2 * pairs:2].set(sink + moved)
    return sizes[jax.random.permutation(jax.random.fold_in(stream_key, 2), number_of)]


def centred(key, extent, spread, limit, pieces=(), held_as=jnp.bfloat16):
    array = jax.random.normal(key, extent, jnp.float32) * spread
    if len(pieces) > 0:
        array = level_of(key, extent, pieces, -0.22, 0.18) * array
    return jnp.clip(array, min=-limit, max=limit).astype(held_as)


def setup_inputs(seed: int = 0) -> dict:
    splits = jax.random.split(jax.random.key(seed), 6)
    queries = draw_queries(jax.random.fold_in(splits[5], 71), 0)
    keys = draw_keys(jax.random.fold_in(splits[5], 71), 0)
    values = centred(splits[2], (TOKENS, KV_HEADS * HEAD_DIM), 1.0, 6.0, ((0, 256),))
    grad_out = centred(splits[3], (TOKENS, HEADS * HEAD_DIM), 1.0, 6.0, ((0, 256),))
    doc_ids = jnp.searchsorted(jnp.cumsum(uneven(splits[4], DOCS, TOKENS, SEQ, 2)), jnp.arange(TOKENS), side="right").astype(jnp.int32)
    return {"queries": queries, "keys": keys, "values": values, "grad_out": grad_out, "doc_ids": doc_ids}


def head_backward(query, grad, key_all, value_all, allowed):
    score_scale = 1.0 / math.sqrt(HEAD_DIM)
    scores = jnp.dot(query, key_all.T, preferred_element_type=jnp.float32) * score_scale
    scores = jnp.where(allowed, scores, -1e+30)
    row_max = lax.optimization_barrier(jnp.max(scores, axis=1, keepdims=True))
    exp_terms = jnp.where(allowed, jnp.exp(scores - row_max), 0.0)
    soft_weights = exp_terms / lax.optimization_barrier(jnp.sum(exp_terms, axis=1, keepdims=True))
    weights_low = soft_weights.astype(jnp.bfloat16)
    grad_weights = jnp.dot(grad, value_all.T, preferred_element_type=jnp.float32)
    row_delta = lax.optimization_barrier(jnp.sum(soft_weights * grad_weights, axis=1, keepdims=True))
    grad_scores = (soft_weights * (grad_weights - row_delta)).astype(jnp.bfloat16)
    query_grad = (jnp.dot(grad_scores, key_all, preferred_element_type=jnp.float32) * score_scale).astype(jnp.bfloat16)
    key_grad = jnp.dot(grad_scores.T, query, preferred_element_type=jnp.float32) * score_scale
    value_grad = jnp.dot(weights_low.T, grad, preferred_element_type=jnp.float32)
    return (query_grad, key_grad, value_grad)

def group_backward(items):
    query, grad, key_own, value_own, key_prev, value_prev, ids_own, ids_prev = items
    key_all = jnp.concatenate([key_prev, key_own], axis=0)
    value_all = jnp.concatenate([value_prev, value_own], axis=0)
    ids_all = jnp.concatenate([ids_prev, ids_own], axis=0)
    key_pos = jnp.arange(2 * SEQ) - SEQ
    positions = jnp.arange(SEQ)
    allowed = (ids_own[:, None] == ids_all[None, :]) & (key_pos[None, :] <= positions[:, None])
    ratio = HEADS // KV_HEADS

    def one_head(head):
        shared = head // ratio
        return head_backward(query[:, head], grad[:, head], key_all[:, shared], value_all[:, shared], allowed)
    query_grad, key_grad, value_grad = lax.map(one_head, jnp.arange(HEADS))
    key_grad = key_grad.reshape(KV_HEADS, ratio, 2 * SEQ, HEAD_DIM).sum(axis=1)
    value_grad = value_grad.reshape(KV_HEADS, ratio, 2 * SEQ, HEAD_DIM).sum(axis=1)
    return (query_grad, key_grad, value_grad)

def reference(queries, keys, values, grad_out, doc_ids):
    groups = TOKENS // SEQ
    query_all = queries.reshape(groups, SEQ, HEADS, HEAD_DIM)
    grad_all = grad_out.reshape(groups, SEQ, HEADS, HEAD_DIM)
    key_own = keys.reshape(groups, SEQ, KV_HEADS, HEAD_DIM)
    value_own = values.reshape(groups, SEQ, KV_HEADS, HEAD_DIM)
    ids_own = doc_ids.reshape(groups, SEQ)
    key_prev = jnp.concatenate([jnp.zeros_like(key_own[:1]), key_own[:-1]], axis=0)
    value_prev = jnp.concatenate([jnp.zeros_like(value_own[:1]), value_own[:-1]], axis=0)
    ids_prev = jnp.concatenate([jnp.zeros_like(ids_own[:1]) - 1, ids_own[:-1]], axis=0)
    query_grad, key_grad, value_grad = lax.map(group_backward, (query_all, grad_all, key_own, value_own, key_prev, value_prev, ids_own, ids_prev))
    key_total = key_grad[:, :, SEQ:] + jnp.concatenate([key_grad[1:, :, :SEQ], jnp.zeros_like(key_grad[:1, :, :SEQ])], axis=0)
    value_total = value_grad[:, :, SEQ:] + jnp.concatenate([value_grad[1:, :, :SEQ], jnp.zeros_like(value_grad[:1, :, :SEQ])], axis=0)
    out_queries = query_grad.transpose(0, 2, 1, 3).reshape(TOKENS, HEADS * HEAD_DIM)
    out_keys = key_total.transpose(0, 2, 1, 3).reshape(TOKENS, KV_HEADS * HEAD_DIM).astype(jnp.bfloat16)
    out_values = value_total.transpose(0, 2, 1, 3).reshape(TOKENS, KV_HEADS * HEAD_DIM).astype(jnp.bfloat16)
    return (out_queries, out_keys, out_values)
```

```python
import functools
import math

import jax
import jax.numpy as jnp
from jax import lax
from jax.experimental import pallas as pl
from jax.experimental.pallas import tpu as pltpu
from jax.sharding import PartitionSpec as P

HEADS = 16
KV_HEADS = 4
HEAD_DIM = 128
RATIO = HEADS // KV_HEADS
SIDE = 4
TOK = 128
QUARTER = SIDE * TOK
BACK = 4
KEYS = (BACK + 1) * QUARTER
TILE = 256
TILES = KEYS // TILE
SCALE = 1.0 / math.sqrt(HEAD_DIM)
EXP2_SCALE = SCALE * math.log2(math.e)
MASKED = -1e30
MESH = pl.DeviceIdType.MESH
F32 = jnp.float32
BF16 = jnp.bfloat16


def tile_rows(tile):
    if tile == 0:
        return 0, TILE
    if tile == TILES - 1:
        return QUARTER - TILE, TILE
    return 0, QUARTER


def kernel(
    groups,
    q_ref, g_ref, k_ref, v_ref, id_ref,
    dq_ref, dk_ref, dv_ref,
    q_all, g_all, k_all, v_all, id_all, kt_all, idk_all,
    e_all, dp_all, m_all, l_all, ed_all, delta_all,
    dqt, dk_sum, dv_sum, dq_out, dkv_out, dkv_in, dkv_last,
    loc_sem, xs, xr, ys, yr, os, orr, qs, qr, ks, kr,
):
    grp = lax.axis_index("grp")
    sp = lax.axis_index("sp")
    y = sp // SIDE
    x = lax.rem(sp, SIDE)
    total = groups * SIDE
    quarter = grp * SIDE + y

    def side(o):
        other = lax.rem(x + o, SIDE)
        return {"sp": y * SIDE + other}, other

    def along(o):
        other = lax.rem(quarter + o + total, total)
        return {"grp": other // SIDE, "sp": lax.rem(other, SIDE) * SIDE + x}

    barrier = pltpu.get_barrier_semaphore()
    for o in range(1, SIDE):
        pl.semaphore_signal(barrier, inc=1, device_id=side(o)[0], device_id_type=MESH)
    for o in range(1, BACK + 1):
        pl.semaphore_signal(barrier, inc=1, device_id=along(o), device_id_type=MESH)
        pl.semaphore_signal(barrier, inc=1, device_id=along(-o), device_id_type=MESH)
    pl.semaphore_wait(barrier, SIDE - 1 + 2 * BACK)

    own = BACK * QUARTER
    my_rows = pl.ds(pl.multiple_of(x * TOK, TOK), TOK)
    my_keys = pl.ds(pl.multiple_of(own + x * TOK, TOK), TOK)

    def columns(head):
        return pl.ds(pl.multiple_of(head * HEAD_DIM, HEAD_DIM), HEAD_DIM)

    def remote(src, dst, send, recv, device):
        return pltpu.make_async_remote_copy(
            src_ref=src, dst_ref=dst, send_sem=send, recv_sem=recv, device_id=device, device_id_type=MESH
        )

    def kv_side(o):
        device, other = side(o)
        at = o - 1
        return [
            remote(k_ref.at[:, columns(other)], k_all.at[my_keys], xs.at[0, at], xr.at[0, at], device),
            remote(v_ref.at[:, columns(other)], v_all.at[my_keys], xs.at[1, at], xr.at[1, at], device),
            remote(id_ref, id_all.at[BACK * SIDE + x], xs.at[2, at], xr.at[2, at], device),
        ]

    def qg_side(h, o):
        device, other = side(o)
        at = o - 1
        cols = columns(other * RATIO + h)
        return [
            remote(q_ref.at[:, cols], q_all.at[h, my_rows], xs.at[3 + h, at], xr.at[3 + h, at], device),
            remote(g_ref.at[:, cols], g_all.at[h, my_rows], xs.at[7 + h, at], xr.at[7 + h, at], device),
        ]

    def kv_local():
        return [
            pltpu.make_async_copy(k_ref.at[:, columns(x)], k_all.at[my_keys], loc_sem.at[0]),
            pltpu.make_async_copy(v_ref.at[:, columns(x)], v_all.at[my_keys], loc_sem.at[1]),
            pltpu.make_async_copy(id_ref, id_all.at[BACK * SIDE + x], loc_sem.at[2]),
        ]

    def qg_local(h):
        cols = columns(x * RATIO + h)
        return [
            pltpu.make_async_copy(q_ref.at[:, cols], q_all.at[h, my_rows], loc_sem.at[3 + h]),
            pltpu.make_async_copy(g_ref.at[:, cols], g_all.at[h, my_rows], loc_sem.at[7 + h]),
        ]

    def keys_of(back):
        return pl.ds((BACK - back) * QUARTER, QUARTER)

    def kv_along(back):
        device = along(back)
        at = back - 1
        return [
            remote(k_all.at[keys_of(0)], k_all.at[keys_of(back)], ys.at[0, at], yr.at[0, at], device),
            remote(v_all.at[keys_of(0)], v_all.at[keys_of(back)], ys.at[1, at], yr.at[1, at], device),
            remote(
                id_all.at[pl.ds(BACK * SIDE, SIDE)],
                id_all.at[pl.ds((BACK - back) * SIDE, SIDE)],
                ys.at[2, at],
                yr.at[2, at],
                device,
            ),
        ]

    def dkv_along(back):
        device = along(-back)
        at = back - 1
        return [
            remote(dkv_out.at[at, i], dkv_in.at[at, i], os.at[i, at], orr.at[i, at], device) for i in range(2)
        ]

    def dq_side(h, o):
        device, other = side(o)
        rows = pl.ds(pl.multiple_of(other * TOK, TOK), TOK)
        return remote(
            dq_out.at[h, rows], dq_ref.at[:, columns(x * RATIO + h)], qs.at[h, o - 1], qr.at[h, o - 1], device
        )

    def dq_local(h):
        return pltpu.make_async_copy(dq_out.at[h, my_rows], dq_ref.at[:, columns(x * RATIO + h)], loc_sem.at[11 + h])

    def dkv_side(i, o):
        device, other = side(o)
        rows = pl.ds(pl.multiple_of(other * TOK, TOK), TOK)
        out = (dk_ref, dv_ref)[i]
        return remote(dkv_last.at[i, rows], out.at[:, columns(x)], ks.at[i, o - 1], kr.at[i, o - 1], device)

    def dkv_local(i):
        out = (dk_ref, dv_ref)[i]
        return pltpu.make_async_copy(dkv_last.at[i, my_rows], out.at[:, columns(x)], loc_sem.at[15 + i])

    for o in range(1, SIDE):
        for copy in kv_side(o):
            copy.start()
    for copy in kv_local():
        copy.start()
    for h in range(RATIO):
        for o in range(1, SIDE):
            for copy in qg_side(h, o):
                copy.start()
        for copy in qg_local(h):
            copy.start()

    for copy in kv_local():
        copy.wait()
    for o in range(1, SIDE):
        for copy in kv_side(o):
            copy.wait_recv()
    for back in (2, 1, 3, 4):
        for copy in kv_along(back):
            copy.start()

    row_at = lax.broadcasted_iota(jnp.int32, (TOK, TOK), 0)
    col_at = lax.broadcasted_iota(jnp.int32, (TOK, TOK), 1)
    ones = jnp.ones((TOK, TOK), BF16)

    def spread_ids(back):
        first = (BACK - back) * SIDE
        for i in range(SIDE):
            ids = jnp.broadcast_to(id_all[first + i].astype(F32), (TOK, TOK))
            diagonal = jnp.where(row_at == col_at, ids, 0.0).astype(BF16)
            idk_all[pl.ds((first + i) * TOK, TOK), :] = jnp.dot(diagonal, ones, preferred_element_type=F32)
        keys = k_all[keys_of(back), :]
        kt_all[:, keys_of(back)] = keys.astype(F32).T.astype(BF16)

    def first_pass(h, tile):
        row, count = tile_rows(tile)
        keys = pl.ds(tile * TILE, TILE)
        rows = pl.ds(row, count)
        key = k_all[keys, :]
        scores = lax.dot_general(
            key, q_all[h, rows, :], (((1,), (1,)), ((), ())), preferred_element_type=F32
        )
        idk = idk_all[keys, :]
        parts = []
        for c in range(count // TOK):
            idq = id_all[BACK * SIDE + row // TOK + c].astype(F32)
            allowed = idk == idq
            key_first = tile * TILE - own
            row_first = row + c * TOK
            if key_first + TILE - 1 > row_first:
                key_pos = key_first + lax.broadcasted_iota(jnp.int32, (TILE, TOK), 0)
                row_pos = row_first + lax.broadcasted_iota(jnp.int32, (TILE, TOK), 1)
                allowed = allowed & (key_pos <= row_pos)
            parts.append(jnp.where(allowed, scores[:, c * TOK : (c + 1) * TOK] * EXP2_SCALE, MASKED))
        scores = jnp.concatenate(parts, axis=1)
        top = jnp.max(scores, axis=0, keepdims=True)
        terms = jnp.exp2(scores - top)
        dp = lax.dot_general(
            v_all[keys, :], g_all[h, rows, :], (((1,), (1,)), ((), ())), preferred_element_type=F32
        )
        e_all[h, tile, :, rows] = terms
        dp_all[h, tile, :, rows] = dp
        m_all[h, tile, :, rows] = top
        l_all[h, tile, :, rows] = jnp.sum(terms, axis=0, keepdims=True)
        ed_all[h, tile, :, rows] = jnp.sum(terms * dp, axis=0, keepdims=True)

    spread_ids(0)
    for back in (0, 4, 1, 3, 2):
        if back > 0:
            for copy in kv_along(back):
                copy.wait_recv()
            spread_ids(back)

        @pl.loop(0, RATIO)
        def _(h, back=back):
            if back == 0:
                for copy in qg_local(h):
                    copy.wait()
                for o in range(1, SIDE):
                    for copy in qg_side(h, o):
                        copy.wait_recv()
            for tile in (2 * (BACK - back), 2 * (BACK - back) + 1):
                first_pass(h, tile)

    @pl.loop(0, RATIO)
    def _(h):
        for half in range(QUARTER // TILE):
            rows = pl.ds(half * TILE, TILE)
            tiles = [t for t in range(TILES) if not (t == 0 and half == 1) and not (t == TILES - 1 and half == 0)]
            tops = [m_all[h, t, :, rows] for t in tiles]
            top = functools.reduce(jnp.maximum, tops)
            weights = [jnp.exp2(one - top) for one in tops]
            total_l = sum(w * l_all[h, t, :, rows] for w, t in zip(weights, tiles))
            total_ed = sum(w * ed_all[h, t, :, rows] for w, t in zip(weights, tiles))
            inverse = 1.0 / total_l
            delta_all[h, :, rows] = total_ed * inverse
            for w, t in zip(weights, tiles):
                m_all[h, t, :, rows] = w * inverse
        dqt[h] = jnp.zeros((HEAD_DIM, QUARTER), F32)

    def second_pass(h, tile, fresh):
        row, count = tile_rows(tile)
        keys = pl.ds(tile * TILE, TILE)
        rows = pl.ds(row, count)
        probs = e_all[h, tile, :, rows] * m_all[h, tile, :, rows]
        ds = (probs * (dp_all[h, tile, :, rows] - delta_all[h, :, rows])).astype(BF16)
        low = probs.astype(BF16)
        dk = jnp.dot(ds, q_all[h, rows, :], preferred_element_type=F32)
        dv = jnp.dot(low, g_all[h, rows, :], preferred_element_type=F32)
        dqt[h, :, rows] += jnp.dot(kt_all[:, keys], ds, preferred_element_type=F32)
        at = pl.ds((tile % 2) * TILE, TILE)
        dk_sum[at, :] += dk
        dv_sum[at, :] += dv

    for back in (2, 1, 3, 4, 0):
        dk_sum[...] = jnp.zeros_like(dk_sum)
        dv_sum[...] = jnp.zeros_like(dv_sum)

        @pl.loop(0, RATIO)
        def _(h, back=back):
            for tile in (2 * (BACK - back), 2 * (BACK - back) + 1):
                second_pass(h, tile, None)
            if back == 0:
                dq_out[h] = (dqt[h] * SCALE).T.astype(BF16)
                for o in range(1, SIDE):
                    dq_side(h, o).start()
                dq_local(h).start()

        if back > 0:
            dkv_out[back - 1, 0] = (dk_sum[...] * SCALE).astype(BF16)
            dkv_out[back - 1, 1] = dv_sum[...].astype(BF16)
            for copy in dkv_along(back):
                copy.start()

    for back in range(1, BACK + 1):
        for copy in dkv_along(back):
            copy.wait_recv()
    for i in range(2):
        one = dk_sum[...] * SCALE if i == 0 else dv_sum[...]
        for back in range(1, BACK + 1):
            one = one + dkv_in[back - 1, i].astype(F32)
        dkv_last[i] = one.astype(BF16)
        for o in range(1, SIDE):
            dkv_side(i, o).start()
        dkv_local(i).start()

    for i in range(2):
        for o in range(1, SIDE):
            dkv_side(i, o).wait()
        dkv_local(i).wait()
    for h in range(RATIO):
        for o in range(1, SIDE):
            dq_side(h, o).wait()
            for copy in qg_side(h, o):
                copy.wait_send()
        dq_local(h).wait()
    for o in range(1, SIDE):
        for copy in kv_side(o):
            copy.wait_send()
    for back in range(1, BACK + 1):
        for copy in kv_along(back):
            copy.wait_send()
        for copy in dkv_along(back):
            copy.wait_send()


def body(groups, queries, keys, values, grad_out, doc_ids):
    dma = pltpu.SemaphoreType.DMA
    return pl.pallas_call(
        functools.partial(kernel, groups),
        out_shape=(
            jax.ShapeDtypeStruct((TOK, HEADS * HEAD_DIM), BF16),
            jax.ShapeDtypeStruct((TOK, KV_HEADS * HEAD_DIM), BF16),
            jax.ShapeDtypeStruct((TOK, KV_HEADS * HEAD_DIM), BF16),
        ),
        in_specs=[pl.BlockSpec(memory_space=pl.ANY)] * 5,
        out_specs=[pl.BlockSpec(memory_space=pl.ANY)] * 3,
        scratch_shapes=[
            pltpu.VMEM((RATIO, QUARTER, HEAD_DIM), BF16),
            pltpu.VMEM((RATIO, QUARTER, HEAD_DIM), BF16),
            pltpu.VMEM((KEYS, HEAD_DIM), BF16),
            pltpu.VMEM((KEYS, HEAD_DIM), BF16),
            pltpu.VMEM(((BACK + 1) * SIDE, 1, TOK), jnp.int32),
            pltpu.VMEM((HEAD_DIM, KEYS), BF16),
            pltpu.VMEM((KEYS, TOK), F32),
            pltpu.VMEM((RATIO, TILES, TILE, QUARTER), F32),
            pltpu.VMEM((RATIO, TILES, TILE, QUARTER), F32),
            pltpu.VMEM((RATIO, TILES, 1, QUARTER), F32),
            pltpu.VMEM((RATIO, TILES, 1, QUARTER), F32),
            pltpu.VMEM((RATIO, TILES, 1, QUARTER), F32),
            pltpu.VMEM((RATIO, 1, QUARTER), F32),
            pltpu.VMEM((RATIO, HEAD_DIM, QUARTER), F32),
            pltpu.VMEM((QUARTER, HEAD_DIM), F32),
            pltpu.VMEM((QUARTER, HEAD_DIM), F32),
            pltpu.VMEM((RATIO, QUARTER, HEAD_DIM), BF16),
            pltpu.VMEM((BACK, 2, QUARTER, HEAD_DIM), BF16),
            pltpu.VMEM((BACK, 2, QUARTER, HEAD_DIM), BF16),
            pltpu.VMEM((2, QUARTER, HEAD_DIM), BF16),
            dma((17,)),
            dma((11, SIDE - 1)),
            dma((11, SIDE - 1)),
            dma((3, BACK)),
            dma((3, BACK)),
            dma((2, BACK)),
            dma((2, BACK)),
            dma((RATIO, SIDE - 1)),
            dma((RATIO, SIDE - 1)),
            dma((2, SIDE - 1)),
            dma((2, SIDE - 1)),
        ],
        compiler_params=pltpu.CompilerParams(
            collective_id=0, has_side_effects=True, vmem_limit_bytes=60 * 1024 * 1024
        ),
    )(queries, grad_out, keys, values, doc_ids.reshape(1, TOK))


def solution(mesh):
    return jax.shard_map(
        functools.partial(body, mesh.shape["grp"]),
        mesh=mesh,
        in_specs=(
            P(("grp", "sp"), None),
            P(("grp", "sp"), None),
            P(("grp", "sp"), None),
            P(("grp", "sp"), None),
            P(("grp", "sp")),
        ),
        out_specs=(P(("grp", "sp"), None), P(("grp", "sp"), None), P(("grp", "sp"), None)),
        check_vma=False,
    )
```

```python
import functools
import math

import jax
import jax.numpy as jnp
from jax import lax
from jax.experimental import pallas as pl
from jax.experimental.pallas import tpu as pltpu
from jax.sharding import PartitionSpec as P

HEADS = 16
KV_HEADS = 4
HEAD_DIM = 128
RATIO = HEADS // KV_HEADS
SIDE = 4
TOK = 128
QUARTER = SIDE * TOK
BACK = 4
KEYS = (BACK + 1) * QUARTER
TILE = 256
TILES = KEYS // TILE
SCALE = 1.0 / math.sqrt(HEAD_DIM)
EXP2_SCALE = SCALE * math.log2(math.e)
MASKED = -1e30
MESH = pl.DeviceIdType.MESH
F32 = jnp.float32
BF16 = jnp.bfloat16


def tile_rows(tile):
    if tile == 0:
        return 0, TILE
    if tile == TILES - 1:
        return QUARTER - TILE, TILE
    return 0, QUARTER


def kernel(
    groups,
    q_ref, g_ref, k_ref, v_ref, id_ref,
    dq_ref, dk_ref, dv_ref,
    q_all, g_all, kv_all, id_all, kt_all, idk_all,
    e_all, dp_all, m_all, l_all, ed_all, delta_all,
    dqt, dk_sum, dv_sum, dq_out, dkv_out, dkv_in, dkv_last,
    loc_sem, xs, xr, ys, yr, os, orr, qs, qr, ks, kr,
):
    grp = lax.axis_index("grp")
    sp = lax.axis_index("sp")
    y = sp // SIDE
    x = lax.rem(sp, SIDE)
    total = groups * SIDE
    quarter = grp * SIDE + y

    def side(o):
        other = lax.rem(x + o, SIDE)
        return {"sp": y * SIDE + other}, other

    def along(o):
        other = lax.rem(quarter + o + total, total)
        return {"grp": other // SIDE, "sp": lax.rem(other, SIDE) * SIDE + x}

    def plane(o):
        return {"sp": lax.rem(y + o, SIDE) * SIDE + x}

    def next_group(o):
        return {"grp": lax.rem(grp + o, groups)}

    barrier = pltpu.get_barrier_semaphore()
    for o in range(1, SIDE):
        pl.semaphore_signal(barrier, inc=1, device_id=side(o)[0], device_id_type=MESH)
        pl.semaphore_signal(barrier, inc=1, device_id=plane(o), device_id_type=MESH)
    for o in (1, groups - 1):
        pl.semaphore_signal(barrier, inc=1, device_id=next_group(o), device_id_type=MESH)
    pl.semaphore_wait(barrier, 2 * SIDE)

    own = BACK * QUARTER
    my_rows = pl.ds(pl.multiple_of(x * TOK, TOK), TOK)
    my_keys = pl.ds(pl.multiple_of(own + x * TOK, TOK), TOK)

    def columns(head):
        return pl.ds(pl.multiple_of(head * HEAD_DIM, HEAD_DIM), HEAD_DIM)

    def remote(src, dst, send, recv, device):
        return pltpu.make_async_remote_copy(
            src_ref=src, dst_ref=dst, send_sem=send, recv_sem=recv, device_id=device, device_id_type=MESH
        )

    def kv_side(o):
        device, other = side(o)
        at = o - 1
        return [
            remote(k_ref.at[:, columns(other)], kv_all.at[0, my_keys], xs.at[0, at], xr.at[0, at], device),
            remote(v_ref.at[:, columns(other)], kv_all.at[1, my_keys], xs.at[1, at], xr.at[1, at], device),
            remote(id_ref, id_all.at[BACK * SIDE + x], xs.at[2, at], xr.at[2, at], device),
        ]

    def qg_side(h, o):
        device, other = side(o)
        at = o - 1
        cols = columns(other * RATIO + h)
        return [
            remote(q_ref.at[:, cols], q_all.at[h, my_rows], xs.at[3 + h, at], xr.at[3 + h, at], device),
            remote(g_ref.at[:, cols], g_all.at[h, my_rows], xs.at[7 + h, at], xr.at[7 + h, at], device),
        ]

    def kv_local():
        return [
            pltpu.make_async_copy(k_ref.at[:, columns(x)], kv_all.at[0, my_keys], loc_sem.at[0]),
            pltpu.make_async_copy(v_ref.at[:, columns(x)], kv_all.at[1, my_keys], loc_sem.at[1]),
            pltpu.make_async_copy(id_ref, id_all.at[BACK * SIDE + x], loc_sem.at[2]),
        ]

    def qg_local(h):
        cols = columns(x * RATIO + h)
        return [
            pltpu.make_async_copy(q_ref.at[:, cols], q_all.at[h, my_rows], loc_sem.at[3 + h]),
            pltpu.make_async_copy(g_ref.at[:, cols], g_all.at[h, my_rows], loc_sem.at[7 + h]),
        ]

    def keys_of(back):
        return pl.ds((BACK - back) * QUARTER, QUARTER)

    def kv_along(back, o, source=0):
        device = next_group(1) if back == BACK else plane(back)
        first = lax.rem(x + SIDE - o, SIDE) * TOK
        src = pl.ds(pl.multiple_of((BACK - source) * QUARTER + first, TOK), TOK)
        dst = pl.ds(pl.multiple_of((BACK - back) * QUARTER + first, TOK), TOK)
        return remote(kv_all.at[:, src], kv_all.at[:, dst], ys.at[o, back - 1], yr.at[o, back - 1], device)

    def id_along(back, source=0):
        device = next_group(1) if back == BACK else plane(back)
        src = pl.ds((BACK - source) * SIDE, SIDE)
        dst = pl.ds((BACK - back) * SIDE, SIDE)
        return remote(id_all.at[src], id_all.at[dst], ys.at[SIDE, back - 1], yr.at[SIDE, back - 1], device)

    def dkv_along(back):
        device = along(-back)
        at = back - 1
        return [
            remote(dkv_out.at[at, i], dkv_in.at[at, i], os.at[i, at], orr.at[i, at], device) for i in range(2)
        ]

    def dq_side(h, o):
        device, other = side(o)
        rows = pl.ds(pl.multiple_of(other * TOK, TOK), TOK)
        return remote(
            dq_out.at[h, rows], dq_ref.at[:, columns(x * RATIO + h)], qs.at[h, o - 1], qr.at[h, o - 1], device
        )

    def dq_local(h):
        return pltpu.make_async_copy(dq_out.at[h, my_rows], dq_ref.at[:, columns(x * RATIO + h)], loc_sem.at[11 + h])

    def dkv_side(i, o):
        device, other = side(o)
        rows = pl.ds(pl.multiple_of(other * TOK, TOK), TOK)
        out = (dk_ref, dv_ref)[i]
        return remote(dkv_last.at[i, rows], out.at[:, columns(x)], ks.at[i, o - 1], kr.at[i, o - 1], device)

    def dkv_local(i):
        out = (dk_ref, dv_ref)[i]
        return pltpu.make_async_copy(dkv_last.at[i, my_rows], out.at[:, columns(x)], loc_sem.at[15 + i])

    for o in range(1, SIDE):
        for copy in kv_side(o):
            copy.start()
    for copy in kv_local():
        copy.start()

    def hand_on(start):
        start(BACK)
        for back in range(1, BACK):

            @pl.when(y + back < SIDE)
            def _(back=back):
                start(back)

    def start_qg(h):
        for o in range(1, SIDE):
            for copy in qg_side(h, o):
                copy.start()
        for copy in qg_local(h):
            copy.start()

    for copy in kv_local():
        copy.wait()
    hand_on(lambda back: kv_along(back, 0).start())
    start_qg(0)
    for o in (1, 3, 2):
        for copy in kv_side(o):
            copy.wait_recv()
        hand_on(lambda back, o=o: kv_along(back, o).start())
    hand_on(lambda back: id_along(back).start())
    for h in range(1, RATIO):
        start_qg(h)

    row_at = lax.broadcasted_iota(jnp.int32, (TOK, TOK), 0)
    col_at = lax.broadcasted_iota(jnp.int32, (TOK, TOK), 1)
    ones = jnp.ones((TOK, TOK), BF16)

    def spread_ids(back):
        first = (BACK - back) * SIDE
        for i in range(SIDE):
            ids = jnp.broadcast_to(id_all[first + i].astype(F32), (TOK, TOK))
            diagonal = jnp.where(row_at == col_at, ids, 0.0).astype(BF16)
            idk_all[pl.ds((first + i) * TOK, TOK), :] = jnp.dot(diagonal, ones, preferred_element_type=F32)
        keys = kv_all[0, keys_of(back), :]
        kt_all[:, keys_of(back)] = keys.astype(F32).T.astype(BF16)

    def first_pass(h, tile):
        row, count = tile_rows(tile)
        keys = pl.ds(tile * TILE, TILE)
        rows = pl.ds(row, count)
        key = kv_all[0, keys, :]
        scores = lax.dot_general(
            key, q_all[h, rows, :], (((1,), (1,)), ((), ())), preferred_element_type=F32
        )
        idk = idk_all[keys, :]
        parts = []
        for c in range(count // TOK):
            idq = id_all[BACK * SIDE + row // TOK + c].astype(F32)
            allowed = idk == idq
            key_first = tile * TILE - own
            row_first = row + c * TOK
            if key_first + TILE - 1 > row_first:
                key_pos = key_first + lax.broadcasted_iota(jnp.int32, (TILE, TOK), 0)
                row_pos = row_first + lax.broadcasted_iota(jnp.int32, (TILE, TOK), 1)
                allowed = allowed & (key_pos <= row_pos)
            parts.append(jnp.where(allowed, scores[:, c * TOK : (c + 1) * TOK] * EXP2_SCALE, MASKED))
        scores = jnp.concatenate(parts, axis=1)
        top = jnp.max(scores, axis=0, keepdims=True)
        terms = jnp.exp2(scores - top)
        dp = lax.dot_general(
            kv_all[1, keys, :], g_all[h, rows, :], (((1,), (1,)), ((), ())), preferred_element_type=F32
        )
        e_all[h, tile, :, rows] = terms
        dp_all[h, tile, :, rows] = dp
        m_all[h, tile, :, rows] = top
        l_all[h, tile, :, rows] = jnp.sum(terms, axis=0, keepdims=True)
        ed_all[h, tile, :, rows] = jnp.sum(terms * dp, axis=0, keepdims=True)

    spread_ids(0)

    def hand_back(start):
        for back in range(1, BACK):

            @pl.when(y + back >= SIDE)
            def _(back=back):
                start(back)

    for o in (0, 1, 3, 2):
        kv_along(BACK, o).wait_recv()
        hand_back(lambda back, o=o: kv_along(back, o, BACK).start())
    id_along(BACK).wait_recv()
    hand_back(lambda back: id_along(back, BACK).start())

    for back in (0, 4, 1, 3, 2):
        if back > 0:
            if back < BACK:
                for o in range(SIDE):
                    kv_along(back, o).wait_recv()
                id_along(back).wait_recv()
            spread_ids(back)

        @pl.loop(0, RATIO)
        def _(h, back=back):
            if back == 0:
                for copy in qg_local(h):
                    copy.wait()
                for o in range(1, SIDE):
                    for copy in qg_side(h, o):
                        copy.wait_recv()
            for tile in (2 * (BACK - back), 2 * (BACK - back) + 1):
                first_pass(h, tile)

    @pl.loop(0, RATIO)
    def _(h):
        for half in range(QUARTER // TILE):
            rows = pl.ds(half * TILE, TILE)
            tiles = [t for t in range(TILES) if not (t == 0 and half == 1) and not (t == TILES - 1 and half == 0)]
            tops = [m_all[h, t, :, rows] for t in tiles]
            top = functools.reduce(jnp.maximum, tops)
            weights = [jnp.exp2(one - top) for one in tops]
            total_l = sum(w * l_all[h, t, :, rows] for w, t in zip(weights, tiles))
            total_ed = sum(w * ed_all[h, t, :, rows] for w, t in zip(weights, tiles))
            inverse = 1.0 / total_l
            delta_all[h, :, rows] = total_ed * inverse
            for w, t in zip(weights, tiles):
                m_all[h, t, :, rows] = w * inverse
        dqt[h] = jnp.zeros((HEAD_DIM, QUARTER), F32)

    def second_pass(h, tile, fresh):
        row, count = tile_rows(tile)
        keys = pl.ds(tile * TILE, TILE)
        rows = pl.ds(row, count)
        probs = e_all[h, tile, :, rows] * m_all[h, tile, :, rows]
        ds = (probs * (dp_all[h, tile, :, rows] - delta_all[h, :, rows])).astype(BF16)
        low = probs.astype(BF16)
        dk = jnp.dot(ds, q_all[h, rows, :], preferred_element_type=F32)
        dv = jnp.dot(low, g_all[h, rows, :], preferred_element_type=F32)
        dqt[h, :, rows] += jnp.dot(kt_all[:, keys], ds, preferred_element_type=F32)
        at = pl.ds((tile % 2) * TILE, TILE)
        dk_sum[at, :] += dk
        dv_sum[at, :] += dv

    for back in (2, 1, 3, 4, 0):
        dk_sum[...] = jnp.zeros_like(dk_sum)
        dv_sum[...] = jnp.zeros_like(dv_sum)

        @pl.loop(0, RATIO)
        def _(h, back=back):
            for tile in (2 * (BACK - back), 2 * (BACK - back) + 1):
                second_pass(h, tile, None)
            if back == 0:
                dq_out[h] = (dqt[h] * SCALE).T.astype(BF16)
                for o in range(1, SIDE):
                    dq_side(h, o).start()
                dq_local(h).start()

        if back > 0:
            dkv_out[back - 1, 0] = (dk_sum[...] * SCALE).astype(BF16)
            dkv_out[back - 1, 1] = dv_sum[...].astype(BF16)
            for copy in dkv_along(back):
                copy.start()

    for back in range(1, BACK + 1):
        for copy in dkv_along(back):
            copy.wait_recv()
    for i in range(2):
        one = dk_sum[...] * SCALE if i == 0 else dv_sum[...]
        for back in range(1, BACK + 1):
            one = one + dkv_in[back - 1, i].astype(F32)
        dkv_last[i] = one.astype(BF16)
        for o in range(1, SIDE):
            dkv_side(i, o).start()
        dkv_local(i).start()

    for i in range(2):
        for o in range(1, SIDE):
            dkv_side(i, o).wait()
        dkv_local(i).wait()
    for h in range(RATIO):
        for o in range(1, SIDE):
            dq_side(h, o).wait()
            for copy in qg_side(h, o):
                copy.wait_send()
        dq_local(h).wait()
    for o in range(1, SIDE):
        for copy in kv_side(o):
            copy.wait_send()
    for back in range(1, BACK + 1):
        for o in range(SIDE):
            kv_along(back, o).wait_send()
        id_along(back).wait_send()
        for copy in dkv_along(back):
            copy.wait_send()


def copy_kernel(*refs):
    count = (len(refs) - 2) // 3
    slabs = []
    for source, target, held in zip(refs[:count], refs[count : 2 * count], refs[2 * count : 3 * count]):
        for first in range(0, source.shape[1], 4 * HEAD_DIM):
            cols = pl.ds(first, 4 * HEAD_DIM)
            slabs.append((source.at[:, cols], held.at[:, cols], target.at[:, cols]))
    read, write = refs[-2:]
    ins = [pltpu.make_async_copy(a, b, read.at[n]) for n, (a, b, _) in enumerate(slabs)]
    outs = [pltpu.make_async_copy(b, c, write.at[n]) for n, (_, b, c) in enumerate(slabs)]
    for copy in ins:
        copy.start()
    for one, two in zip(ins, outs):
        one.wait()
        two.start()
    for copy in outs:
        copy.wait()


def copied(arrays):
    count = len(arrays)
    slabs = sum(a.shape[1] // (4 * HEAD_DIM) for a in arrays)
    return pl.pallas_call(
        copy_kernel,
        out_shape=tuple(jax.ShapeDtypeStruct(a.shape, a.dtype) for a in arrays),
        in_specs=[pl.BlockSpec(memory_space=pl.ANY)] * count,
        out_specs=[pl.BlockSpec(memory_space=pl.ANY)] * count,
        scratch_shapes=[pltpu.VMEM(a.shape, a.dtype) for a in arrays]
        + [pltpu.SemaphoreType.DMA((slabs,)), pltpu.SemaphoreType.DMA((slabs,))],
    )(*arrays)


def body(groups, queries, keys, values, grad_out, doc_ids):
    dma = pltpu.SemaphoreType.DMA
    outs = pl.pallas_call(
        functools.partial(kernel, groups),
        out_shape=(
            jax.ShapeDtypeStruct((TOK, HEADS * HEAD_DIM), BF16),
            jax.ShapeDtypeStruct((TOK, KV_HEADS * HEAD_DIM), BF16),
            jax.ShapeDtypeStruct((TOK, KV_HEADS * HEAD_DIM), BF16),
        ),
        in_specs=[pl.BlockSpec(memory_space=pl.ANY)] * 5,
        out_specs=[pl.BlockSpec(memory_space=pl.ANY)] * 3,
        scratch_shapes=[
            pltpu.VMEM((RATIO, QUARTER, HEAD_DIM), BF16),
            pltpu.VMEM((RATIO, QUARTER, HEAD_DIM), BF16),
            pltpu.VMEM((2, KEYS, HEAD_DIM), BF16),
            pltpu.VMEM(((BACK + 1) * SIDE, 1, TOK), jnp.int32),
            pltpu.VMEM((HEAD_DIM, KEYS), BF16),
            pltpu.VMEM((KEYS, TOK), F32),
            pltpu.VMEM((RATIO, TILES, TILE, QUARTER), F32),
            pltpu.VMEM((RATIO, TILES, TILE, QUARTER), F32),
            pltpu.VMEM((RATIO, TILES, 1, QUARTER), F32),
            pltpu.VMEM((RATIO, TILES, 1, QUARTER), F32),
            pltpu.VMEM((RATIO, TILES, 1, QUARTER), F32),
            pltpu.VMEM((RATIO, 1, QUARTER), F32),
            pltpu.VMEM((RATIO, HEAD_DIM, QUARTER), F32),
            pltpu.VMEM((QUARTER, HEAD_DIM), F32),
            pltpu.VMEM((QUARTER, HEAD_DIM), F32),
            pltpu.VMEM((RATIO, QUARTER, HEAD_DIM), BF16),
            pltpu.VMEM((BACK, 2, QUARTER, HEAD_DIM), BF16),
            pltpu.VMEM((BACK, 2, QUARTER, HEAD_DIM), BF16),
            pltpu.VMEM((2, QUARTER, HEAD_DIM), BF16),
            dma((17,)),
            dma((11, SIDE - 1)),
            dma((11, SIDE - 1)),
            dma((SIDE + 1, BACK)),
            dma((SIDE + 1, BACK)),
            dma((2, BACK)),
            dma((2, BACK)),
            dma((RATIO, SIDE - 1)),
            dma((RATIO, SIDE - 1)),
            dma((2, SIDE - 1)),
            dma((2, SIDE - 1)),
        ],
        compiler_params=pltpu.CompilerParams(
            collective_id=0, has_side_effects=True, vmem_limit_bytes=60 * 1024 * 1024
        ),
    )(queries, grad_out, keys, values, doc_ids.reshape(1, TOK))
    return copied(outs)


def solution(mesh):
    return jax.shard_map(
        functools.partial(body, mesh.shape["grp"]),
        mesh=mesh,
        in_specs=(
            P(("grp", "sp"), None),
            P(("grp", "sp"), None),
            P(("grp", "sp"), None),
            P(("grp", "sp"), None),
            P(("grp", "sp")),
        ),
        out_specs=(P(("grp", "sp"), None), P(("grp", "sp"), None), P(("grp", "sp"), None)),
        check_vma=False,
    )
```

```python
import functools
import math

import jax
import jax.numpy as jnp
from jax import lax
from jax.experimental import pallas as pl
from jax.experimental.pallas import tpu as pltpu
from jax.sharding import PartitionSpec as P

HEADS = 16
KV_HEADS = 4
HEAD_DIM = 128
RATIO = HEADS // KV_HEADS
SIDE = 4
TOK = 128
QUARTER = SIDE * TOK
BACK = 4
KEYS = (BACK + 1) * QUARTER
TILE = 256
TILES = KEYS // TILE
SCALE = 1.0 / math.sqrt(HEAD_DIM)
EXP2_SCALE = SCALE * math.log2(math.e)
MASKED = -1e30
ORDER = (2, 1, 3, 4, 0)
MESH = pl.DeviceIdType.MESH
F32 = jnp.float32
BF16 = jnp.bfloat16


def tile_rows(tile):
    if tile == 0:
        return 0, TILE
    if tile == TILES - 1:
        return QUARTER - TILE, TILE
    return 0, QUARTER


def kernel(
    groups,
    q_ref, g_ref, k_ref, v_ref, id_ref,
    dq_ref, dk_ref, dv_ref,
    q_all, g_all, kv_all, id_all, kt_all, idk_all,
    e_all, dp_all, m_all, l_all, ed_all, delta_all,
    dqt, dk_sum, dv_sum, dq_out, dkv_out, dkv_in, dkv_last,
    loc_sem, xs, xr, ys, yr, os, orr, qs, qr, ks, kr,
):
    grp = lax.axis_index("grp")
    sp = lax.axis_index("sp")
    y = sp // SIDE
    x = lax.rem(sp, SIDE)
    total = groups * SIDE
    quarter = grp * SIDE + y

    def side(o):
        other = lax.rem(x + o, SIDE)
        return {"sp": y * SIDE + other}, other

    def along(o):
        other = lax.rem(quarter + o + total, total)
        return {"grp": other // SIDE, "sp": lax.rem(other, SIDE) * SIDE + x}

    def plane(o):
        return {"sp": lax.rem(y + o, SIDE) * SIDE + x}

    def next_group(o):
        return {"grp": lax.rem(grp + o, groups)}

    barrier = pltpu.get_barrier_semaphore()
    for o in range(1, SIDE):
        pl.semaphore_signal(barrier, inc=1, device_id=side(o)[0], device_id_type=MESH)
        pl.semaphore_signal(barrier, inc=1, device_id=plane(o), device_id_type=MESH)
    for o in (1, groups - 1):
        pl.semaphore_signal(barrier, inc=1, device_id=next_group(o), device_id_type=MESH)
    pl.semaphore_wait(barrier, 2 * SIDE)

    own = BACK * QUARTER
    my_rows = pl.ds(pl.multiple_of(x * TOK, TOK), TOK)
    my_keys = pl.ds(pl.multiple_of(own + x * TOK, TOK), TOK)

    def columns(head):
        return pl.ds(pl.multiple_of(head * HEAD_DIM, HEAD_DIM), HEAD_DIM)

    def remote(src, dst, send, recv, device):
        return pltpu.make_async_remote_copy(
            src_ref=src, dst_ref=dst, send_sem=send, recv_sem=recv, device_id=device, device_id_type=MESH
        )

    def kv_side(i, o):
        device, other = side(o)
        source = (k_ref, v_ref)[i]
        return remote(source.at[:, columns(other)], kv_all.at[i, my_keys], xs.at[i, o - 1], xr.at[i, o - 1], device)

    def id_side(o):
        device, _ = side(o)
        return remote(id_ref, id_all.at[BACK * SIDE + x], xs.at[2, o - 1], xr.at[2, o - 1], device)

    def qg_side(i, h, o):
        device, other = side(o)
        source, target = ((q_ref, q_all), (g_ref, g_all))[i]
        at = 3 + i * RATIO + h
        cols = columns(other * RATIO + h)
        return remote(source.at[:, cols], target.at[h, my_rows], xs.at[at, o - 1], xr.at[at, o - 1], device)

    def kv_local(i):
        source = (k_ref, v_ref)[i]
        return pltpu.make_async_copy(source.at[:, columns(x)], kv_all.at[i, my_keys], loc_sem.at[i])

    def id_local():
        return pltpu.make_async_copy(id_ref, id_all.at[BACK * SIDE + x], loc_sem.at[2])

    def qg_local(i, h):
        source, target = ((q_ref, q_all), (g_ref, g_all))[i]
        return pltpu.make_async_copy(
            source.at[:, columns(x * RATIO + h)], target.at[h, my_rows], loc_sem.at[3 + i * RATIO + h]
        )

    def keys_of(back):
        return pl.ds((BACK - back) * QUARTER, QUARTER)

    def kv_along(i, back, o, source=0):
        device = next_group(1) if back == BACK else plane(back)
        first = lax.rem(x + SIDE - o, SIDE) * TOK
        src = pl.ds(pl.multiple_of((BACK - source) * QUARTER + first, TOK), TOK)
        dst = pl.ds(pl.multiple_of((BACK - back) * QUARTER + first, TOK), TOK)
        at = i * SIDE + o
        return remote(kv_all.at[i, src], kv_all.at[i, dst], ys.at[at, back - 1], yr.at[at, back - 1], device)

    def id_along(back, source=0):
        device = next_group(1) if back == BACK else plane(back)
        src = pl.ds((BACK - source) * SIDE, SIDE)
        dst = pl.ds((BACK - back) * SIDE, SIDE)
        return remote(id_all.at[src], id_all.at[dst], ys.at[2 * SIDE, back - 1], yr.at[2 * SIDE, back - 1], device)

    def dkv_along(i, back):
        at = back - 1
        return remote(dkv_out.at[at, i], dkv_in.at[at, i], os.at[i, at], orr.at[i, at], along(-back))

    def dq_side(h, o):
        device, other = side(o)
        rows = pl.ds(pl.multiple_of(other * TOK, TOK), TOK)
        return remote(
            dq_out.at[h, rows], dq_ref.at[:, columns(x * RATIO + h)], qs.at[h, o - 1], qr.at[h, o - 1], device
        )

    def dq_local(h):
        return pltpu.make_async_copy(dq_out.at[h, my_rows], dq_ref.at[:, columns(x * RATIO + h)], loc_sem.at[11 + h])

    def dkv_side(i, o):
        device, other = side(o)
        rows = pl.ds(pl.multiple_of(other * TOK, TOK), TOK)
        out = (dk_ref, dv_ref)[i]
        return remote(dkv_last.at[i, rows], out.at[:, columns(x)], ks.at[i, o - 1], kr.at[i, o - 1], device)

    def dkv_local(i):
        out = (dk_ref, dv_ref)[i]
        return pltpu.make_async_copy(dkv_last.at[i, my_rows], out.at[:, columns(x)], loc_sem.at[15 + i])

    def later(start):
        for back in range(1, BACK):

            @pl.when(y + back < SIDE)
            def _(back=back):
                start(back)

    def earlier(start):
        for back in range(1, BACK):

            @pl.when(y + back >= SIDE)
            def _(back=back):
                start(back)

    def start_qg(i):
        for h in range(RATIO):
            for o in range(1, SIDE):
                qg_side(i, h, o).start()
            qg_local(i, h).start()

    chunks = (0, 1, 3, 2)

    def wait_chunk(i, o):
        if o == 0:
            kv_local(i).wait()
        else:
            kv_side(i, o).wait_recv()

    for o in range(1, SIDE):
        kv_side(0, o).start()
    kv_local(0).start()
    for o in range(1, SIDE):
        id_side(o).start()
    id_local().start()
    for o in range(1, SIDE):
        kv_side(1, o).start()
    kv_local(1).start()

    for o in chunks:
        wait_chunk(0, o)
        kv_along(0, BACK, o).start()
        later(lambda back, o=o: kv_along(0, back, o).start())
        if o == 0:
            start_qg(0)
    id_local().wait()
    for o in range(1, SIDE):
        id_side(o).wait_recv()
    id_along(BACK).start()
    later(lambda back: id_along(back).start())
    for o in chunks:
        wait_chunk(1, o)
        kv_along(1, BACK, o).start()
    start_qg(1)

    row_at = lax.broadcasted_iota(jnp.int32, (TOK, TOK), 0)
    col_at = lax.broadcasted_iota(jnp.int32, (TOK, TOK), 1)
    ones = jnp.ones((TOK, TOK), BF16)

    def spread_ids(back):
        first = (BACK - back) * SIDE
        for i in range(SIDE):
            ids = jnp.broadcast_to(id_all[first + i].astype(F32), (TOK, TOK))
            diagonal = jnp.where(row_at == col_at, ids, 0.0).astype(BF16)
            idk_all[pl.ds((first + i) * TOK, TOK), :] = jnp.dot(diagonal, ones, preferred_element_type=F32)
        keys = kv_all[0, keys_of(back), :]
        kt_all[:, keys_of(back)] = keys.astype(F32).T.astype(BF16)

    def first_pass(h, tile):
        row, count = tile_rows(tile)
        keys = pl.ds(tile * TILE, TILE)
        rows = pl.ds(row, count)
        across = (((1,), (1,)), ((), ()))
        scores = lax.dot_general(kv_all[0, keys, :], q_all[h, rows, :], across, preferred_element_type=F32)
        idk = idk_all[keys, :]
        parts = []
        for c in range(count // TOK):
            allowed = idk == id_all[BACK * SIDE + row // TOK + c].astype(F32)
            key_first = tile * TILE - own
            row_first = row + c * TOK
            if key_first + TILE - 1 > row_first:
                key_pos = key_first + lax.broadcasted_iota(jnp.int32, (TILE, TOK), 0)
                row_pos = row_first + lax.broadcasted_iota(jnp.int32, (TILE, TOK), 1)
                allowed = allowed & (key_pos <= row_pos)
            parts.append(jnp.where(allowed, scores[:, c * TOK : (c + 1) * TOK] * EXP2_SCALE, MASKED))
        scores = jnp.concatenate(parts, axis=1)
        top = jnp.max(scores, axis=0, keepdims=True)
        terms = jnp.exp2(scores - top)
        e_all[h, tile, :, rows] = terms
        m_all[h, tile, :, rows] = top
        l_all[h, tile, :, rows] = jnp.sum(terms, axis=0, keepdims=True)

    for o in chunks:
        kv_along(0, BACK, o).wait_recv()
        earlier(lambda back, o=o: kv_along(0, back, o, BACK).start())
        if o == 0:
            for one in chunks:
                later(lambda back, one=one: kv_along(1, back, one).start())
    id_along(BACK).wait_recv()
    earlier(lambda back: id_along(back, BACK).start())

    def tiles_of(back):
        return (2 * (BACK - back), 2 * (BACK - back) + 1)

    spread_ids(0)
    spread_ids(BACK)
    for back in (0, 4, 1, 3, 2):
        if 0 < back < BACK:
            for o in range(SIDE):
                kv_along(0, back, o).wait_recv()
            id_along(back).wait_recv()
            spread_ids(back)

        @pl.loop(0, RATIO, unroll=True)
        def _(h, back=back):
            if back == 0:
                qg_local(0, h).wait()
                for o in range(1, SIDE):
                    qg_side(0, h, o).wait_recv()
            for tile in tiles_of(back):
                first_pass(h, tile)

        if back == BACK:
            for o in chunks:
                kv_along(1, BACK, o).wait_recv()
                earlier(lambda back, o=o: kv_along(1, back, o, BACK).start())

    halves = range(QUARTER // TILE)

    def tiles_for(half):
        return [t for t in range(TILES) if not (t == 0 and half == 1) and not (t == TILES - 1 and half == 0)]

    @pl.loop(0, RATIO, unroll=True)
    def _(h):
        for half in halves:
            rows = pl.ds(half * TILE, TILE)
            tiles = tiles_for(half)
            tops = [m_all[h, t, :, rows] for t in tiles]
            top = functools.reduce(jnp.maximum, tops)
            weights = [jnp.exp2(one - top) for one in tops]
            inverse = 1.0 / sum(w * l_all[h, t, :, rows] for w, t in zip(weights, tiles))
            for w, t in zip(weights, tiles):
                m_all[h, t, :, rows] = w * inverse
        dqt[h] = jnp.zeros((HEAD_DIM, QUARTER), F32)

    def value_pass(h, tile):
        row, count = tile_rows(tile)
        rows = pl.ds(row, count)
        low = (e_all[h, tile, :, rows] * m_all[h, tile, :, rows]).astype(BF16)
        at = pl.ds((tile % 2) * TILE, TILE)
        dv_sum[at, :] += jnp.dot(low, g_all[h, rows, :], preferred_element_type=F32)

    for h in range(RATIO):
        qg_local(1, h).wait()
        for o in range(1, SIDE):
            qg_side(1, h, o).wait_recv()
    for back in ORDER:
        dv_sum[...] = jnp.zeros_like(dv_sum)

        @pl.loop(0, RATIO, unroll=True)
        def _(h, back=back):
            for tile in tiles_of(back):
                value_pass(h, tile)

        if back > 0:
            dkv_out[back - 1, 1] = dv_sum[...].astype(BF16)
            dkv_along(1, back).start()

    def delta_pass(h, tile):
        row, count = tile_rows(tile)
        keys = pl.ds(tile * TILE, TILE)
        rows = pl.ds(row, count)
        across = (((1,), (1,)), ((), ()))
        dp = lax.dot_general(kv_all[1, keys, :], g_all[h, rows, :], across, preferred_element_type=F32)
        dp_all[h, tile, :, rows] = dp
        ed_all[h, tile, :, rows] = jnp.sum(e_all[h, tile, :, rows] * dp, axis=0, keepdims=True)

    for back in (0, 4, 1, 3, 2):
        if 0 < back < BACK:
            for o in range(SIDE):
                kv_along(1, back, o).wait_recv()

        @pl.loop(0, RATIO, unroll=True)
        def _(h, back=back):
            for tile in tiles_of(back):
                delta_pass(h, tile)

    @pl.loop(0, RATIO, unroll=True)
    def _(h):
        for half in halves:
            rows = pl.ds(half * TILE, TILE)
            delta_all[h, :, rows] = sum(m_all[h, t, :, rows] * ed_all[h, t, :, rows] for t in tiles_for(half))

    def key_pass(h, tile):
        row, count = tile_rows(tile)
        keys = pl.ds(tile * TILE, TILE)
        rows = pl.ds(row, count)
        probs = e_all[h, tile, :, rows] * m_all[h, tile, :, rows]
        ds = (probs * (dp_all[h, tile, :, rows] - delta_all[h, :, rows])).astype(BF16)
        dqt[h, :, rows] += jnp.dot(kt_all[:, keys], ds, preferred_element_type=F32)
        at = pl.ds((tile % 2) * TILE, TILE)
        dk_sum[at, :] += jnp.dot(ds, q_all[h, rows, :], preferred_element_type=F32)

    for back in ORDER:
        dk_sum[...] = jnp.zeros_like(dk_sum)

        @pl.loop(0, RATIO, unroll=True)
        def _(h, back=back):
            for tile in tiles_of(back):
                key_pass(h, tile)
            if back == 0:
                dq_out[h] = (dqt[h] * SCALE).T.astype(BF16)
                for o in range(1, SIDE):
                    dq_side(h, o).start()
                dq_local(h).start()

        if back > 0:
            dkv_out[back - 1, 0] = (dk_sum[...] * SCALE).astype(BF16)
            dkv_along(0, back).start()

    for i in (1, 0):
        one = dk_sum[...] * SCALE if i == 0 else dv_sum[...]
        for back in range(1, BACK + 1):
            dkv_along(i, back).wait_recv()
            one = one + dkv_in[back - 1, i].astype(F32)
        dkv_last[i] = one.astype(BF16)
        for o in range(1, SIDE):
            dkv_side(i, o).start()
        dkv_local(i).start()

    for i in range(2):
        for o in range(1, SIDE):
            dkv_side(i, o).wait()
            kv_side(i, o).wait_send()
            for h in range(RATIO):
                qg_side(i, h, o).wait_send()
        dkv_local(i).wait()
        for back in range(1, BACK + 1):
            for o in range(SIDE):
                kv_along(i, back, o).wait_send()
            dkv_along(i, back).wait_send()
    for h in range(RATIO):
        for o in range(1, SIDE):
            dq_side(h, o).wait()
        dq_local(h).wait()
    for o in range(1, SIDE):
        id_side(o).wait_send()
    for back in range(1, BACK + 1):
        id_along(back).wait_send()


def copy_kernel(*refs):
    count = (len(refs) - 2) // 3
    slabs = []
    for source, target, held in zip(refs[:count], refs[count : 2 * count], refs[2 * count : 3 * count]):
        for first in range(0, source.shape[1], 4 * HEAD_DIM):
            cols = pl.ds(first, 4 * HEAD_DIM)
            slabs.append((source.at[:, cols], held.at[:, cols], target.at[:, cols]))
    read, write = refs[-2:]
    ins = [pltpu.make_async_copy(a, b, read.at[n]) for n, (a, b, _) in enumerate(slabs)]
    outs = [pltpu.make_async_copy(b, c, write.at[n]) for n, (_, b, c) in enumerate(slabs)]
    for copy in ins:
        copy.start()
    for one, two in zip(ins, outs):
        one.wait()
        two.start()
    for copy in outs:
        copy.wait()


def copied(arrays):
    count = len(arrays)
    slabs = sum(a.shape[1] // (4 * HEAD_DIM) for a in arrays)
    return pl.pallas_call(
        copy_kernel,
        out_shape=tuple(jax.ShapeDtypeStruct(a.shape, a.dtype) for a in arrays),
        in_specs=[pl.BlockSpec(memory_space=pl.ANY)] * count,
        out_specs=[pl.BlockSpec(memory_space=pl.ANY)] * count,
        scratch_shapes=[pltpu.VMEM(a.shape, a.dtype) for a in arrays]
        + [pltpu.SemaphoreType.DMA((slabs,)), pltpu.SemaphoreType.DMA((slabs,))],
    )(*arrays)


def body(groups, queries, keys, values, grad_out, doc_ids):
    dma = pltpu.SemaphoreType.DMA
    outs = pl.pallas_call(
        functools.partial(kernel, groups),
        out_shape=(
            jax.ShapeDtypeStruct((TOK, HEADS * HEAD_DIM), BF16),
            jax.ShapeDtypeStruct((TOK, KV_HEADS * HEAD_DIM), BF16),
            jax.ShapeDtypeStruct((TOK, KV_HEADS * HEAD_DIM), BF16),
        ),
        in_specs=[pl.BlockSpec(memory_space=pl.ANY)] * 5,
        out_specs=[pl.BlockSpec(memory_space=pl.ANY)] * 3,
        scratch_shapes=[
            pltpu.VMEM((RATIO, QUARTER, HEAD_DIM), BF16),
            pltpu.VMEM((RATIO, QUARTER, HEAD_DIM), BF16),
            pltpu.VMEM((2, KEYS, HEAD_DIM), BF16),
            pltpu.VMEM(((BACK + 1) * SIDE, 1, TOK), jnp.int32),
            pltpu.VMEM((HEAD_DIM, KEYS), BF16),
            pltpu.VMEM((KEYS, TOK), F32),
            pltpu.VMEM((RATIO, TILES, TILE, QUARTER), F32),
            pltpu.VMEM((RATIO, TILES, TILE, QUARTER), F32),
            pltpu.VMEM((RATIO, TILES, 1, QUARTER), F32),
            pltpu.VMEM((RATIO, TILES, 1, QUARTER), F32),
            pltpu.VMEM((RATIO, TILES, 1, QUARTER), F32),
            pltpu.VMEM((RATIO, 1, QUARTER), F32),
            pltpu.VMEM((RATIO, HEAD_DIM, QUARTER), F32),
            pltpu.VMEM((QUARTER, HEAD_DIM), F32),
            pltpu.VMEM((QUARTER, HEAD_DIM), F32),
            pltpu.VMEM((RATIO, QUARTER, HEAD_DIM), BF16),
            pltpu.VMEM((BACK, 2, QUARTER, HEAD_DIM), BF16),
            pltpu.VMEM((BACK, 2, QUARTER, HEAD_DIM), BF16),
            pltpu.VMEM((2, QUARTER, HEAD_DIM), BF16),
            dma((17,)),
            dma((11, SIDE - 1)),
            dma((11, SIDE - 1)),
            dma((2 * SIDE + 1, BACK)),
            dma((2 * SIDE + 1, BACK)),
            dma((2, BACK)),
            dma((2, BACK)),
            dma((RATIO, SIDE - 1)),
            dma((RATIO, SIDE - 1)),
            dma((2, SIDE - 1)),
            dma((2, SIDE - 1)),
        ],
        compiler_params=pltpu.CompilerParams(
            collective_id=0, has_side_effects=True, vmem_limit_bytes=60 * 1024 * 1024
        ),
    )(queries, grad_out, keys, values, doc_ids.reshape(1, TOK))
    return copied(outs)


def solution(mesh):
    return jax.shard_map(
        functools.partial(body, mesh.shape["grp"]),
        mesh=mesh,
        in_specs=(
            P(("grp", "sp"), None),
            P(("grp", "sp"), None),
            P(("grp", "sp"), None),
            P(("grp", "sp"), None),
            P(("grp", "sp")),
        ),
        out_specs=(P(("grp", "sp"), None), P(("grp", "sp"), None), P(("grp", "sp"), None)),
        check_vma=False,
    )
```

```python
import functools
import math

import jax
import jax.numpy as jnp
from jax import lax
from jax.experimental import pallas as pl
from jax.experimental.pallas import tpu as pltpu
from jax.sharding import PartitionSpec as P

HEADS = 16
KV_HEADS = 4
HEAD_DIM = 128
RATIO = HEADS // KV_HEADS
SIDE = 4
TOK = 128
QUARTER = SIDE * TOK
BACK = 4
KEYS = (BACK + 1) * QUARTER
TILE = 256
TILES = KEYS // TILE
SCALE = 1.0 / math.sqrt(HEAD_DIM)
EXP2_SCALE = SCALE * math.log2(math.e)
MASKED = -1e30
ORDER = (3, 2, 1, 4, 0)
MESH = pl.DeviceIdType.MESH
F32 = jnp.float32
BF16 = jnp.bfloat16


def tile_rows(tile):
    if tile == 0:
        return 0, TILE
    if tile == TILES - 1:
        return QUARTER - TILE, TILE
    return 0, QUARTER


def kernel(
    groups,
    q_ref, g_ref, k_ref, v_ref, id_ref,
    dq_ref, dk_ref, dv_ref,
    q_all, g_all, kv_all, id_all, kt_all, idk_all,
    e_all, dp_all, m_all, l_all, ed_all, delta_all,
    dqt, dk_sum, dv_sum, dq_out, dkv_out, dkv_in, dkv_last,
    loc_sem, sent, side_in, along_in, back_in,
):
    grp = lax.axis_index("grp")
    sp = lax.axis_index("sp")
    y = sp // SIDE
    x = lax.rem(sp, SIDE)
    total = groups * SIDE
    quarter = grp * SIDE + y

    def side(o):
        other = lax.rem(x + o, SIDE)
        return {"sp": y * SIDE + other}, other

    def along(o):
        other = lax.rem(quarter + o + total, total)
        return {"grp": other // SIDE, "sp": lax.rem(other, SIDE) * SIDE + x}

    def plane(o):
        return {"sp": lax.rem(y + o, SIDE) * SIDE + x}

    def next_group(o):
        return {"grp": lax.rem(grp + o, groups)}

    barrier = pltpu.get_barrier_semaphore()
    for o in range(1, SIDE):
        pl.semaphore_signal(barrier, inc=1, device_id=side(o)[0], device_id_type=MESH)
        pl.semaphore_signal(barrier, inc=1, device_id=plane(o), device_id_type=MESH)
    for o in (1, groups - 1):
        pl.semaphore_signal(barrier, inc=1, device_id=next_group(o), device_id_type=MESH)

    own = BACK * QUARTER
    my_rows = pl.ds(pl.multiple_of(x * TOK, TOK), TOK)
    my_keys = pl.ds(pl.multiple_of(own + x * TOK, TOK), TOK)

    def columns(head):
        return pl.ds(pl.multiple_of(head * HEAD_DIM, HEAD_DIM), HEAD_DIM)

    def remote(src, dst, send, recv, device):
        return pltpu.make_async_remote_copy(
            src_ref=src, dst_ref=dst, send_sem=send, recv_sem=recv, device_id=device, device_id_type=MESH
        )

    def kv_side(i, o):
        device, other = side(o)
        source = (k_ref, v_ref)[i]
        return remote(source.at[:, columns(other)], kv_all.at[i, my_keys], sent.at[i], side_in.at[i * SIDE + o], device)

    def id_side(o):
        device, _ = side(o)
        return remote(id_ref, id_all.at[BACK * SIDE + x], sent.at[2], side_in.at[0], device)

    def qg_side(i, h, o):
        device, other = side(o)
        source, target = ((q_ref, q_all), (g_ref, g_all))[i]
        at = 2 * SIDE + i * RATIO + h
        cols = columns(other * RATIO + h)
        return remote(source.at[:, cols], target.at[h, my_rows], sent.at[3 + i], side_in.at[at], device)

    def kv_local(i):
        source = (k_ref, v_ref)[i]
        return pltpu.make_async_copy(source.at[:, columns(x)], kv_all.at[i, my_keys], loc_sem.at[i])

    def id_local():
        return pltpu.make_async_copy(id_ref, id_all.at[BACK * SIDE + x], loc_sem.at[2])

    def qg_local(i, h):
        source, target = ((q_ref, q_all), (g_ref, g_all))[i]
        return pltpu.make_async_copy(
            source.at[:, columns(x * RATIO + h)], target.at[h, my_rows], loc_sem.at[3 + i * RATIO + h]
        )

    def keys_of(back):
        return pl.ds((BACK - back) * QUARTER, QUARTER)

    def kv_along(i, back, o, source=0):
        device = next_group(1) if back == BACK else plane(back)
        first = lax.rem(x + SIDE - o, SIDE) * TOK
        src = pl.ds(pl.multiple_of((BACK - source) * QUARTER + first, TOK), TOK)
        dst = pl.ds(pl.multiple_of((BACK - back) * QUARTER + first, TOK), TOK)
        at = i * 2 * SIDE + (o if back == BACK else SIDE + back)
        return remote(kv_all.at[i, src], kv_all.at[i, dst], sent.at[5 + i], along_in.at[at], device)

    def id_along(back, source=0):
        device = next_group(1) if back == BACK else plane(back)
        src = pl.ds((BACK - source) * SIDE, SIDE)
        dst = pl.ds((BACK - back) * SIDE, SIDE)
        return remote(id_all.at[src], id_all.at[dst], sent.at[7], along_in.at[4 * SIDE + back - 1], device)

    def dkv_along(i, back):
        at = back - 1
        return remote(dkv_out.at[at, i], dkv_in.at[at, i], sent.at[8 + i], back_in.at[i], along(-back))

    def dq_side(h, o):
        device, other = side(o)
        rows = pl.ds(pl.multiple_of(other * TOK, TOK), TOK)
        return remote(
            dq_out.at[h, rows], dq_ref.at[:, columns(x * RATIO + h)], sent.at[10], back_in.at[2], device
        )

    def dq_local(h):
        return pltpu.make_async_copy(dq_out.at[h, my_rows], dq_ref.at[:, columns(x * RATIO + h)], loc_sem.at[11 + h])

    def dkv_side(i, o):
        device, other = side(o)
        rows = pl.ds(pl.multiple_of(other * TOK, TOK), TOK)
        out = (dk_ref, dv_ref)[i]
        return remote(dkv_last.at[i, rows], out.at[:, columns(x)], sent.at[11 + i], back_in.at[3 + i], device)

    def dkv_local(i):
        out = (dk_ref, dv_ref)[i]
        return pltpu.make_async_copy(dkv_last.at[i, my_rows], out.at[:, columns(x)], loc_sem.at[15 + i])

    def later(start):
        for back in range(1, BACK):

            @pl.when(y + back < SIDE)
            def _(back=back):
                start(back)

    def earlier(start):
        for back in range(1, BACK):

            @pl.when(y + back >= SIDE)
            def _(back=back):
                start(back)

    def start_qg(i):
        for h in range(RATIO):
            for o in range(1, SIDE):
                qg_side(i, h, o).start()

    chunks = (0, 1, 3, 2)

    def wait_chunk(i, o):
        if o == 0:
            kv_local(i).wait()
        else:
            kv_side(i, o).wait_recv()

    def arrived(ref, sem):
        pltpu.make_async_copy(ref, ref, sem).wait()

    three = pl.ds(0, (SIDE - 1) * TOK)

    kv_local(0).start()
    id_local().start()
    kv_local(1).start()
    for i in range(2):
        for h in range(RATIO):
            qg_local(i, h).start()
    pl.semaphore_wait(barrier, 2 * SIDE)
    for o in range(1, SIDE):
        kv_side(0, o).start()
    for o in range(1, SIDE):
        id_side(o).start()
    for o in range(1, SIDE):
        kv_side(1, o).start()

    for o in chunks:
        wait_chunk(0, o)
        kv_along(0, BACK, o).start()
        later(lambda back, o=o: kv_along(0, back, o).start())
        if o == 0:
            start_qg(0)
    id_local().wait()
    arrived(id_all.at[pl.ds(0, SIDE - 1)], side_in.at[0])
    id_along(BACK).start()
    later(lambda back: id_along(back).start())
    for o in chunks:
        wait_chunk(1, o)
        kv_along(1, BACK, o).start()
    start_qg(1)

    row_at = lax.broadcasted_iota(jnp.int32, (TOK, TOK), 0)
    col_at = lax.broadcasted_iota(jnp.int32, (TOK, TOK), 1)
    ones = jnp.ones((TOK, TOK), BF16)

    def spread_ids(back):
        first = (BACK - back) * SIDE
        for i in range(SIDE):
            ids = jnp.broadcast_to(id_all[first + i].astype(F32), (TOK, TOK))
            diagonal = jnp.where(row_at == col_at, ids, 0.0).astype(BF16)
            idk_all[pl.ds((first + i) * TOK, TOK), :] = jnp.dot(diagonal, ones, preferred_element_type=F32)
        keys = kv_all[0, keys_of(back), :]
        kt_all[:, keys_of(back)] = keys.astype(F32).T.astype(BF16)

    def first_pass(h, tile):
        row, count = tile_rows(tile)
        keys = pl.ds(tile * TILE, TILE)
        rows = pl.ds(row, count)
        across = (((1,), (1,)), ((), ()))
        scores = lax.dot_general(kv_all[0, keys, :], q_all[h, rows, :], across, preferred_element_type=F32)
        idk = idk_all[keys, :]
        parts = []
        for c in range(count // TOK):
            allowed = idk == id_all[BACK * SIDE + row // TOK + c].astype(F32)
            key_first = tile * TILE - own
            row_first = row + c * TOK
            if key_first + TILE - 1 > row_first:
                key_pos = key_first + lax.broadcasted_iota(jnp.int32, (TILE, TOK), 0)
                row_pos = row_first + lax.broadcasted_iota(jnp.int32, (TILE, TOK), 1)
                allowed = allowed & (key_pos <= row_pos)
            parts.append(jnp.where(allowed, scores[:, c * TOK : (c + 1) * TOK] * EXP2_SCALE, MASKED))
        scores = jnp.concatenate(parts, axis=1)
        top = jnp.max(scores, axis=0, keepdims=True)
        terms = jnp.exp2(scores - top)
        e_all[h, tile, :, rows] = terms
        m_all[h, tile, :, rows] = top
        l_all[h, tile, :, rows] = jnp.sum(terms, axis=0, keepdims=True)

    for o in chunks:
        kv_along(0, BACK, o).wait_recv()
        earlier(lambda back, o=o: kv_along(0, back, o, BACK).start())
        if o == 0:
            for one in chunks:
                later(lambda back, one=one: kv_along(1, back, one).start())
    id_along(BACK).wait_recv()
    earlier(lambda back: id_along(back, BACK).start())

    def tiles_of(back):
        return (2 * (BACK - back), 2 * (BACK - back) + 1)

    spread_ids(0)
    spread_ids(BACK)
    for back in (0, 4, 1, 3, 2):
        if 0 < back < BACK:
            arrived(kv_all.at[0, keys_of(back)], along_in.at[SIDE + back])
            id_along(back).wait_recv()
            spread_ids(back)

        @pl.loop(0, RATIO, unroll=True)
        def _(h, back=back):
            if back == 0:
                qg_local(0, h).wait()
                arrived(q_all.at[h, three], side_in.at[2 * SIDE + h])
            for tile in tiles_of(back):
                first_pass(h, tile)

        if back == BACK:
            for o in chunks:
                kv_along(1, BACK, o).wait_recv()
                earlier(lambda back, o=o: kv_along(1, back, o, BACK).start())

    halves = range(QUARTER // TILE)

    def tiles_for(half):
        return [t for t in range(TILES) if not (t == 0 and half == 1) and not (t == TILES - 1 and half == 0)]

    @pl.loop(0, RATIO, unroll=True)
    def _(h):
        for half in halves:
            rows = pl.ds(half * TILE, TILE)
            tiles = tiles_for(half)
            tops = [m_all[h, t, :, rows] for t in tiles]
            top = functools.reduce(jnp.maximum, tops)
            weights = [jnp.exp2(one - top) for one in tops]
            inverse = 1.0 / sum(w * l_all[h, t, :, rows] for w, t in zip(weights, tiles))
            for w, t in zip(weights, tiles):
                m_all[h, t, :, rows] = w * inverse
        dqt[h] = jnp.zeros((HEAD_DIM, QUARTER), F32)

    def value_pass(h, tile):
        row, count = tile_rows(tile)
        rows = pl.ds(row, count)
        low = (e_all[h, tile, :, rows] * m_all[h, tile, :, rows]).astype(BF16)
        at = pl.ds((tile % 2) * TILE, TILE)
        dv_sum[at, :] += jnp.dot(low, g_all[h, rows, :], preferred_element_type=F32)

    for h in range(RATIO):
        qg_local(1, h).wait()
        arrived(g_all.at[h, three], side_in.at[2 * SIDE + RATIO + h])
    for back in ORDER:
        dv_sum[...] = jnp.zeros_like(dv_sum)

        @pl.loop(0, RATIO, unroll=True)
        def _(h, back=back):
            for tile in tiles_of(back):
                value_pass(h, tile)

        if back > 0:
            dkv_out[back - 1, 1] = dv_sum[...].astype(BF16)
            dkv_along(1, back).start()

    def delta_pass(h, tile):
        row, count = tile_rows(tile)
        keys = pl.ds(tile * TILE, TILE)
        rows = pl.ds(row, count)
        across = (((1,), (1,)), ((), ()))
        dp = lax.dot_general(kv_all[1, keys, :], g_all[h, rows, :], across, preferred_element_type=F32)
        dp_all[h, tile, :, rows] = dp
        ed_all[h, tile, :, rows] = jnp.sum(e_all[h, tile, :, rows] * dp, axis=0, keepdims=True)

    for back in (0, 4, 1, 3, 2):
        if 0 < back < BACK:
            arrived(kv_all.at[1, keys_of(back)], along_in.at[2 * SIDE + SIDE + back])

        @pl.loop(0, RATIO, unroll=True)
        def _(h, back=back):
            for tile in tiles_of(back):
                delta_pass(h, tile)

    @pl.loop(0, RATIO, unroll=True)
    def _(h):
        for half in halves:
            rows = pl.ds(half * TILE, TILE)
            delta_all[h, :, rows] = sum(m_all[h, t, :, rows] * ed_all[h, t, :, rows] for t in tiles_for(half))

    def key_pass(h, tile):
        row, count = tile_rows(tile)
        keys = pl.ds(tile * TILE, TILE)
        rows = pl.ds(row, count)
        probs = e_all[h, tile, :, rows] * m_all[h, tile, :, rows]
        ds = (probs * (dp_all[h, tile, :, rows] - delta_all[h, :, rows])).astype(BF16)
        dqt[h, :, rows] += jnp.dot(kt_all[:, keys], ds, preferred_element_type=F32)
        at = pl.ds((tile % 2) * TILE, TILE)
        dk_sum[at, :] += jnp.dot(ds, q_all[h, rows, :], preferred_element_type=F32)

    for back in ORDER:
        dk_sum[...] = jnp.zeros_like(dk_sum)

        @pl.loop(0, RATIO, unroll=True)
        def _(h, back=back):
            for tile in tiles_of(back):
                key_pass(h, tile)
            if back == 0:
                dq_out[h] = (dqt[h] * SCALE).T.astype(BF16)
                for o in range(1, SIDE):
                    dq_side(h, o).start()
                dq_local(h).start()

        if back > 0:
            dkv_out[back - 1, 0] = (dk_sum[...] * SCALE).astype(BF16)
            dkv_along(0, back).start()

    arrived(id_all.at[pl.ds(0, SIDE - 1)], sent.at[2])
    arrived(id_all.at[pl.ds(0, SIDE * SIDE)], sent.at[7])
    for i in range(2):
        arrived(kv_all.at[i, three], sent.at[i])
        arrived(q_all.at[pl.ds(0, SIDE - 1)], sent.at[3 + i])
        arrived(q_all, sent.at[5 + i])

    for i in (1, 0):
        one = dk_sum[...] * SCALE if i == 0 else dv_sum[...]
        arrived(q_all, back_in.at[i])
        for back in range(1, BACK + 1):
            one = one + dkv_in[back - 1, i].astype(F32)
        dkv_last[i] = one.astype(BF16)
        for o in range(1, SIDE):
            dkv_side(i, o).start()
        dkv_local(i).start()

    arrived(q_all, sent.at[8])
    arrived(q_all, sent.at[9])
    for h in range(RATIO):
        dq_local(h).wait()
    arrived(q_all.at[pl.ds(0, SIDE - 1)], sent.at[10])
    arrived(q_all.at[pl.ds(0, SIDE - 1)], back_in.at[2])
    for i in (1, 0):
        dkv_local(i).wait()
        arrived(dkv_last.at[i, three], sent.at[11 + i])
        arrived(dkv_last.at[i, three], back_in.at[3 + i])


def copy_kernel(*refs):
    count = (len(refs) - 2) // 3
    slabs = []
    for source, target, held in zip(refs[:count], refs[count : 2 * count], refs[2 * count : 3 * count]):
        for first in range(0, source.shape[1], 4 * HEAD_DIM):
            cols = pl.ds(first, 4 * HEAD_DIM)
            slabs.append((source.at[:, cols], held.at[:, cols], target.at[:, cols]))
    read, write = refs[-2:]
    ins = [pltpu.make_async_copy(a, b, read.at[n]) for n, (a, b, _) in enumerate(slabs)]
    outs = [pltpu.make_async_copy(b, c, write.at[n]) for n, (_, b, c) in enumerate(slabs)]
    for copy in ins:
        copy.start()
    for one, two in zip(ins, outs):
        one.wait()
        two.start()
    for copy in outs:
        copy.wait()


def copied(arrays):
    count = len(arrays)
    slabs = sum(a.shape[1] // (4 * HEAD_DIM) for a in arrays)
    return pl.pallas_call(
        copy_kernel,
        out_shape=tuple(jax.ShapeDtypeStruct(a.shape, a.dtype) for a in arrays),
        in_specs=[pl.BlockSpec(memory_space=pl.ANY)] * count,
        out_specs=[pl.BlockSpec(memory_space=pl.ANY)] * count,
        scratch_shapes=[pltpu.VMEM(a.shape, a.dtype) for a in arrays]
        + [pltpu.SemaphoreType.DMA((slabs,)), pltpu.SemaphoreType.DMA((slabs,))],
    )(*arrays)


def body(groups, queries, keys, values, grad_out, doc_ids):
    dma = pltpu.SemaphoreType.DMA
    outs = pl.pallas_call(
        functools.partial(kernel, groups),
        out_shape=(
            jax.ShapeDtypeStruct((TOK, HEADS * HEAD_DIM), BF16),
            jax.ShapeDtypeStruct((TOK, KV_HEADS * HEAD_DIM), BF16),
            jax.ShapeDtypeStruct((TOK, KV_HEADS * HEAD_DIM), BF16),
        ),
        in_specs=[pl.BlockSpec(memory_space=pl.ANY)] * 5,
        out_specs=[pl.BlockSpec(memory_space=pl.ANY)] * 3,
        scratch_shapes=[
            pltpu.VMEM((RATIO, QUARTER, HEAD_DIM), BF16),
            pltpu.VMEM((RATIO, QUARTER, HEAD_DIM), BF16),
            pltpu.VMEM((2, KEYS, HEAD_DIM), BF16),
            pltpu.VMEM(((BACK + 1) * SIDE, 1, TOK), jnp.int32),
            pltpu.VMEM((HEAD_DIM, KEYS), BF16),
            pltpu.VMEM((KEYS, TOK), F32),
            pltpu.VMEM((RATIO, TILES, TILE, QUARTER), F32),
            pltpu.VMEM((RATIO, TILES, TILE, QUARTER), F32),
            pltpu.VMEM((RATIO, TILES, 1, QUARTER), F32),
            pltpu.VMEM((RATIO, TILES, 1, QUARTER), F32),
            pltpu.VMEM((RATIO, TILES, 1, QUARTER), F32),
            pltpu.VMEM((RATIO, 1, QUARTER), F32),
            pltpu.VMEM((RATIO, HEAD_DIM, QUARTER), F32),
            pltpu.VMEM((QUARTER, HEAD_DIM), F32),
            pltpu.VMEM((QUARTER, HEAD_DIM), F32),
            pltpu.VMEM((RATIO, QUARTER, HEAD_DIM), BF16),
            pltpu.VMEM((BACK, 2, QUARTER, HEAD_DIM), BF16),
            pltpu.VMEM((BACK, 2, QUARTER, HEAD_DIM), BF16),
            pltpu.VMEM((2, QUARTER, HEAD_DIM), BF16),
            dma((17,)),
            dma((13,)),
            dma((4 * SIDE,)),
            dma((5 * SIDE,)),
            dma((5,)),
        ],
        compiler_params=pltpu.CompilerParams(
            collective_id=0, has_side_effects=True, vmem_limit_bytes=60 * 1024 * 1024
        ),
    )(queries, grad_out, keys, values, doc_ids.reshape(1, TOK))
    return copied(outs)


def solution(mesh):
    return jax.shard_map(
        functools.partial(body, mesh.shape["grp"]),
        mesh=mesh,
        in_specs=(
            P(("grp", "sp"), None),
            P(("grp", "sp"), None),
            P(("grp", "sp"), None),
            P(("grp", "sp"), None),
            P(("grp", "sp")),
        ),
        out_specs=(P(("grp", "sp"), None), P(("grp", "sp"), None), P(("grp", "sp"), None)),
        check_vma=False,
    )
```

```python
import functools
import math

import jax
import jax.numpy as jnp
from jax import lax
from jax.experimental import pallas as pl
from jax.experimental.pallas import tpu as pltpu
from jax.sharding import PartitionSpec as P

HEADS = 16
KV_HEADS = 4
HEAD_DIM = 128
RATIO = HEADS // KV_HEADS
SIDE = 4
TOK = 128
QUARTER = SIDE * TOK
BACK = 4
KEYS = (BACK + 1) * QUARTER
TILE = 256
TILES = KEYS // TILE
SCALE = 1.0 / math.sqrt(HEAD_DIM)
EXP2_SCALE = SCALE * math.log2(math.e)
MASKED = -1e30
ORDER = (3, 2, 1, 4, 0)
MESH = pl.DeviceIdType.MESH
F32 = jnp.float32
BF16 = jnp.bfloat16


def tile_rows(tile):
    if tile == 0:
        return 0, TILE
    if tile == TILES - 1:
        return QUARTER - TILE, TILE
    return 0, QUARTER


def kernel(
    groups,
    q_ref, g_ref, k_ref, v_ref, id_ref,
    dq_ref, dk_ref, dv_ref,
    q_all, g_all, kv_all, id_all, kt_all, idk_all,
    e_all, dp_all, m_all, l_all, ed_all, delta_all,
    dk_sum, dv_sum, dq_out, dkv_out, dkv_in, dkv_last,
    loc_sem, sent, side_in, along_in, back_in,
):
    grp = lax.axis_index("grp")
    sp = lax.axis_index("sp")
    y = sp // SIDE
    x = lax.rem(sp, SIDE)
    total = groups * SIDE
    quarter = grp * SIDE + y

    def side(o):
        other = lax.rem(x + o, SIDE)
        return {"sp": y * SIDE + other}, other

    def along(o):
        other = lax.rem(quarter + o + total, total)
        return {"grp": other // SIDE, "sp": lax.rem(other, SIDE) * SIDE + x}

    def plane(o):
        return {"sp": lax.rem(y + o, SIDE) * SIDE + x}

    def next_group(o):
        return {"grp": lax.rem(grp + o, groups)}

    barrier = pltpu.get_barrier_semaphore()
    for o in range(1, SIDE):
        pl.semaphore_signal(barrier, inc=1, device_id=side(o)[0], device_id_type=MESH)
        pl.semaphore_signal(barrier, inc=1, device_id=plane(o), device_id_type=MESH)
    for o in (1, groups - 1):
        pl.semaphore_signal(barrier, inc=1, device_id=next_group(o), device_id_type=MESH)

    own = BACK * QUARTER
    my_rows = pl.ds(pl.multiple_of(x * TOK, TOK), TOK)
    my_keys = pl.ds(pl.multiple_of(own + x * TOK, TOK), TOK)

    def columns(head):
        return pl.ds(pl.multiple_of(head * HEAD_DIM, HEAD_DIM), HEAD_DIM)

    def remote(src, dst, send, recv, device):
        return pltpu.make_async_remote_copy(
            src_ref=src, dst_ref=dst, send_sem=send, recv_sem=recv, device_id=device, device_id_type=MESH
        )

    def kv_side(i, o):
        device, other = side(o)
        source = (k_ref, v_ref)[i]
        return remote(source.at[:, columns(other)], kv_all.at[i, my_keys], sent.at[i], side_in.at[i * SIDE + o], device)

    def id_side(o):
        device, _ = side(o)
        return remote(id_ref, id_all.at[BACK * SIDE + x], sent.at[2], side_in.at[0], device)

    def qg_side(i, h, o):
        device, other = side(o)
        source, target = ((q_ref, q_all), (g_ref, g_all))[i]
        at = 2 * SIDE + i * RATIO + h
        cols = columns(other * RATIO + h)
        return remote(source.at[:, cols], target.at[h, my_rows], sent.at[3 + i], side_in.at[at], device)

    def kv_local(i):
        source = (k_ref, v_ref)[i]
        return pltpu.make_async_copy(source.at[:, columns(x)], kv_all.at[i, my_keys], loc_sem.at[i])

    def id_local():
        return pltpu.make_async_copy(id_ref, id_all.at[BACK * SIDE + x], loc_sem.at[2])

    def qg_local(i, h):
        source, target = ((q_ref, q_all), (g_ref, g_all))[i]
        return pltpu.make_async_copy(
            source.at[:, columns(x * RATIO + h)], target.at[h, my_rows], loc_sem.at[3 + i * RATIO + h]
        )

    def keys_of(back):
        return pl.ds((BACK - back) * QUARTER, QUARTER)

    def kv_along(i, back, o, source=0):
        device = next_group(1) if back == BACK else plane(back)
        first = lax.rem(x + SIDE - o, SIDE) * TOK
        src = pl.ds(pl.multiple_of((BACK - source) * QUARTER + first, TOK), TOK)
        dst = pl.ds(pl.multiple_of((BACK - back) * QUARTER + first, TOK), TOK)
        at = i * 2 * SIDE + (o if back == BACK else SIDE + back)
        return remote(kv_all.at[i, src], kv_all.at[i, dst], sent.at[5 + i], along_in.at[at], device)

    def id_along(back, source=0):
        device = next_group(1) if back == BACK else plane(back)
        src = pl.ds((BACK - source) * SIDE, SIDE)
        dst = pl.ds((BACK - back) * SIDE, SIDE)
        return remote(id_all.at[src], id_all.at[dst], sent.at[7], along_in.at[4 * SIDE + back - 1], device)

    def dkv_along(i, back):
        at = back - 1
        return remote(dkv_out.at[at, i], dkv_in.at[at, i], sent.at[8 + i], back_in.at[i], along(-back))

    def dq_side(h, o):
        device, other = side(o)
        rows = pl.ds(pl.multiple_of(other * TOK, TOK), TOK)
        return remote(
            dq_out.at[h, rows], dq_ref.at[:, columns(x * RATIO + h)], sent.at[10], back_in.at[2], device
        )

    def dq_local(h):
        return pltpu.make_async_copy(dq_out.at[h, my_rows], dq_ref.at[:, columns(x * RATIO + h)], loc_sem.at[11 + h])

    def dkv_side(i, o):
        device, other = side(o)
        rows = pl.ds(pl.multiple_of(other * TOK, TOK), TOK)
        out = (dk_ref, dv_ref)[i]
        return remote(dkv_last.at[i, rows], out.at[:, columns(x)], sent.at[11 + i], back_in.at[3 + i], device)

    def dkv_local(i):
        out = (dk_ref, dv_ref)[i]
        return pltpu.make_async_copy(dkv_last.at[i, my_rows], out.at[:, columns(x)], loc_sem.at[15 + i])

    def later(start):
        for back in range(1, BACK):

            @pl.when(y + back < SIDE)
            def _(back=back):
                start(back)

    def earlier(start):
        for back in range(1, BACK):

            @pl.when(y + back >= SIDE)
            def _(back=back):
                start(back)

    def start_qg(i):
        for h in range(RATIO):
            for o in range(1, SIDE):
                qg_side(i, h, o).start()

    chunks = (0, 1, 3, 2)

    def wait_chunk(i, o):
        if o == 0:
            kv_local(i).wait()
        else:
            kv_side(i, o).wait_recv()

    def arrived(ref, sem):
        pltpu.make_async_copy(ref, ref, sem).wait()

    three = pl.ds(0, (SIDE - 1) * TOK)

    kv_local(0).start()
    id_local().start()
    kv_local(1).start()
    for i in range(2):
        for h in range(RATIO):
            qg_local(i, h).start()
    pl.semaphore_wait(barrier, 2 * SIDE)
    for o in range(1, SIDE):
        kv_side(0, o).start()
    for o in range(1, SIDE):
        id_side(o).start()
    for o in range(1, SIDE):
        kv_side(1, o).start()

    for o in chunks:
        wait_chunk(0, o)
        kv_along(0, BACK, o).start()
        later(lambda back, o=o: kv_along(0, back, o).start())
        if o == 0:
            start_qg(0)
    id_local().wait()
    arrived(id_all.at[pl.ds(0, SIDE - 1)], side_in.at[0])
    id_along(BACK).start()
    later(lambda back: id_along(back).start())
    for o in chunks:
        wait_chunk(1, o)
        kv_along(1, BACK, o).start()
        later(lambda back, o=o: kv_along(1, back, o).start())
    start_qg(1)

    row_at = lax.broadcasted_iota(jnp.int32, (TOK, TOK), 0)
    col_at = lax.broadcasted_iota(jnp.int32, (TOK, TOK), 1)
    ones = jnp.ones((TOK, TOK), BF16)

    def spread_ids(back):
        first = (BACK - back) * SIDE
        for i in range(SIDE):
            ids = jnp.broadcast_to(id_all[first + i].astype(F32), (TOK, TOK))
            diagonal = jnp.where(row_at == col_at, ids, 0.0).astype(BF16)
            idk_all[pl.ds((first + i) * TOK, TOK), :] = jnp.dot(diagonal, ones, preferred_element_type=F32)
        keys = kv_all[0, keys_of(back), :]
        kt_all[:, keys_of(back)] = keys.astype(F32).T.astype(BF16)

    def first_pass(h, tile):
        row, count = tile_rows(tile)
        keys = pl.ds(tile * TILE, TILE)
        rows = pl.ds(row, count)
        across = (((1,), (1,)), ((), ()))
        scores = lax.dot_general(kv_all[0, keys, :], q_all[h, rows, :], across, preferred_element_type=F32)
        idk = idk_all[keys, :]
        parts = []
        for c in range(count // TOK):
            allowed = idk == id_all[BACK * SIDE + row // TOK + c].astype(F32)
            key_first = tile * TILE - own
            row_first = row + c * TOK
            if key_first + TILE - 1 > row_first:
                key_pos = key_first + lax.broadcasted_iota(jnp.int32, (TILE, TOK), 0)
                row_pos = row_first + lax.broadcasted_iota(jnp.int32, (TILE, TOK), 1)
                allowed = allowed & (key_pos <= row_pos)
            parts.append(jnp.where(allowed, scores[:, c * TOK : (c + 1) * TOK] * EXP2_SCALE, MASKED))
        scores = jnp.concatenate(parts, axis=1)
        top = jnp.max(scores, axis=0, keepdims=True)
        terms = jnp.exp2(scores - top)
        e_all[h, tile, :, rows] = terms
        m_all[h, tile, :, rows] = top
        l_all[h, tile, :, rows] = jnp.sum(terms, axis=0, keepdims=True)

    for o in chunks:
        kv_along(0, BACK, o).wait_recv()
        earlier(lambda back, o=o: kv_along(0, back, o, BACK).start())
    id_along(BACK).wait_recv()
    earlier(lambda back: id_along(back, BACK).start())

    def tiles_of(back):
        return (2 * (BACK - back), 2 * (BACK - back) + 1)

    spread_ids(0)
    spread_ids(BACK)
    for back in (0, 4, 1, 3, 2):
        if 0 < back < BACK:
            arrived(kv_all.at[0, keys_of(back)], along_in.at[SIDE + back])
            id_along(back).wait_recv()
            spread_ids(back)

        @pl.loop(0, RATIO, unroll=True)
        def _(h, back=back):
            if back == 0:
                qg_local(0, h).wait()
                arrived(q_all.at[h, three], side_in.at[2 * SIDE + h])
            for tile in tiles_of(back):
                first_pass(h, tile)

        if back == BACK:
            for o in chunks:
                kv_along(1, BACK, o).wait_recv()
                earlier(lambda back, o=o: kv_along(1, back, o, BACK).start())

    halves = range(QUARTER // TILE)

    def tiles_for(half):
        return [t for t in range(TILES) if not (t == 0 and half == 1) and not (t == TILES - 1 and half == 0)]

    @pl.loop(0, RATIO, unroll=True)
    def _(h):
        for half in halves:
            rows = pl.ds(half * TILE, TILE)
            tiles = tiles_for(half)
            tops = [m_all[h, t, :, rows] for t in tiles]
            top = functools.reduce(jnp.maximum, tops)
            weights = [jnp.exp2(one - top) for one in tops]
            inverse = 1.0 / sum(w * l_all[h, t, :, rows] for w, t in zip(weights, tiles))
            for w, t in zip(weights, tiles):
                m_all[h, t, :, rows] = w * inverse

    def value_pass(h, tile):
        row, count = tile_rows(tile)
        rows = pl.ds(row, count)
        low = (e_all[h, tile, :, rows] * m_all[h, tile, :, rows]).astype(BF16)
        at = pl.ds((tile % 2) * TILE, TILE)
        dv_sum[at, :] += jnp.dot(low, g_all[h, rows, :], preferred_element_type=F32)

    for h in range(RATIO):
        qg_local(1, h).wait()
        arrived(g_all.at[h, three], side_in.at[2 * SIDE + RATIO + h])
    for back in ORDER:
        dv_sum[...] = jnp.zeros_like(dv_sum)

        @pl.loop(0, RATIO, unroll=True)
        def _(h, back=back):
            for tile in tiles_of(back):
                value_pass(h, tile)

        if back > 0:
            dkv_out[back - 1, 1] = dv_sum[...].astype(BF16)
            dkv_along(1, back).start()

    def delta_pass(h, tile):
        row, count = tile_rows(tile)
        keys = pl.ds(tile * TILE, TILE)
        rows = pl.ds(row, count)
        across = (((1,), (1,)), ((), ()))
        dp = lax.dot_general(kv_all[1, keys, :], g_all[h, rows, :], across, preferred_element_type=F32)
        dp_all[h, tile, :, rows] = dp
        ed_all[h, tile, :, rows] = jnp.sum(e_all[h, tile, :, rows] * dp, axis=0, keepdims=True)

    for back in (0, 4, 1, 3, 2):
        if 0 < back < BACK:
            arrived(kv_all.at[1, keys_of(back)], along_in.at[2 * SIDE + SIDE + back])

        @pl.loop(0, RATIO, unroll=True)
        def _(h, back=back):
            for tile in tiles_of(back):
                delta_pass(h, tile)

    @pl.loop(0, RATIO, unroll=True)
    def _(h):
        for half in halves:
            rows = pl.ds(half * TILE, TILE)
            delta_all[h, :, rows] = sum(m_all[h, t, :, rows] * ed_all[h, t, :, rows] for t in tiles_for(half))

    def key_pass(h, tile):
        row, count = tile_rows(tile)
        keys = pl.ds(tile * TILE, TILE)
        rows = pl.ds(row, count)
        probs = e_all[h, tile, :, rows] * m_all[h, tile, :, rows]
        ds = probs * (dp_all[h, tile, :, rows] - delta_all[h, :, rows])
        dp_all[h, tile, :, rows] = ds
        at = pl.ds((tile % 2) * TILE, TILE)
        dk_sum[at, :] += jnp.dot(ds.astype(BF16), q_all[h, rows, :], preferred_element_type=F32)

    def query_grad(h):
        for half in halves:
            rows = pl.ds(half * TILE, TILE)
            first = half * TILE
            ds = [dp_all[h, t, :, rows].astype(BF16) for t in tiles_for(half)]
            keys = kt_all[:, first : first + len(ds) * TILE]
            dqt = jnp.dot(keys, jnp.concatenate(ds, axis=0), preferred_element_type=F32)
            dq_out[h, rows, :] = (dqt * SCALE).T.astype(BF16)
        for o in range(1, SIDE):
            dq_side(h, o).start()
        dq_local(h).start()

    for back in ORDER:
        dk_sum[...] = jnp.zeros_like(dk_sum)

        @pl.loop(0, RATIO, unroll=True)
        def _(h, back=back):
            for tile in tiles_of(back):
                key_pass(h, tile)

        if back > 0:
            dkv_out[back - 1, 0] = (dk_sum[...] * SCALE).astype(BF16)
            dkv_along(0, back).start()

    for h in range(RATIO):
        query_grad(h)

    arrived(id_all.at[pl.ds(0, SIDE - 1)], sent.at[2])
    arrived(id_all.at[pl.ds(0, SIDE * SIDE)], sent.at[7])
    for i in range(2):
        arrived(kv_all.at[i, three], sent.at[i])
        arrived(q_all.at[pl.ds(0, SIDE - 1)], sent.at[3 + i])
        arrived(q_all, sent.at[5 + i])

    for i in (1, 0):
        one = dk_sum[...] * SCALE if i == 0 else dv_sum[...]
        arrived(q_all, back_in.at[i])
        for back in range(1, BACK + 1):
            one = one + dkv_in[back - 1, i].astype(F32)
        dkv_last[i] = one.astype(BF16)
        for o in range(1, SIDE):
            dkv_side(i, o).start()
        dkv_local(i).start()

    arrived(q_all, sent.at[8])
    arrived(q_all, sent.at[9])
    for h in range(RATIO):
        dq_local(h).wait()
    arrived(q_all.at[pl.ds(0, SIDE - 1)], sent.at[10])
    arrived(q_all.at[pl.ds(0, SIDE - 1)], back_in.at[2])
    for i in (1, 0):
        dkv_local(i).wait()
        arrived(dkv_last.at[i, three], sent.at[11 + i])
        arrived(dkv_last.at[i, three], back_in.at[3 + i])


def copy_kernel(*refs):
    count = (len(refs) - 2) // 3
    slabs = []
    for source, target, held in zip(refs[:count], refs[count : 2 * count], refs[2 * count : 3 * count]):
        for first in range(0, source.shape[1], 2 * HEAD_DIM):
            cols = pl.ds(first, 2 * HEAD_DIM)
            slabs.append((source.at[:, cols], held.at[:, cols], target.at[:, cols]))
    read, write = refs[-2:]
    ins = [pltpu.make_async_copy(a, b, read.at[n]) for n, (a, b, _) in enumerate(slabs)]
    outs = [pltpu.make_async_copy(b, c, write.at[n]) for n, (_, b, c) in enumerate(slabs)]
    for copy in ins:
        copy.start()
    for one, two in zip(ins, outs):
        one.wait()
        two.start()
    for copy in outs:
        copy.wait()


def copied(arrays):
    count = len(arrays)
    slabs = sum(a.shape[1] // (2 * HEAD_DIM) for a in arrays)
    return pl.pallas_call(
        copy_kernel,
        out_shape=tuple(jax.ShapeDtypeStruct(a.shape, a.dtype) for a in arrays),
        in_specs=[pl.BlockSpec(memory_space=pl.ANY)] * count,
        out_specs=[pl.BlockSpec(memory_space=pl.ANY)] * count,
        scratch_shapes=[pltpu.VMEM(a.shape, a.dtype) for a in arrays]
        + [pltpu.SemaphoreType.DMA((slabs,)), pltpu.SemaphoreType.DMA((slabs,))],
    )(*arrays)


def body(groups, queries, keys, values, grad_out, doc_ids):
    dma = pltpu.SemaphoreType.DMA
    outs = pl.pallas_call(
        functools.partial(kernel, groups),
        out_shape=(
            jax.ShapeDtypeStruct((TOK, HEADS * HEAD_DIM), BF16),
            jax.ShapeDtypeStruct((TOK, KV_HEADS * HEAD_DIM), BF16),
            jax.ShapeDtypeStruct((TOK, KV_HEADS * HEAD_DIM), BF16),
        ),
        in_specs=[pl.BlockSpec(memory_space=pl.ANY)] * 5,
        out_specs=[pl.BlockSpec(memory_space=pl.ANY)] * 3,
        scratch_shapes=[
            pltpu.VMEM((RATIO, QUARTER, HEAD_DIM), BF16),
            pltpu.VMEM((RATIO, QUARTER, HEAD_DIM), BF16),
            pltpu.VMEM((2, KEYS, HEAD_DIM), BF16),
            pltpu.VMEM(((BACK + 1) * SIDE, 1, TOK), jnp.int32),
            pltpu.VMEM((HEAD_DIM, KEYS), BF16),
            pltpu.VMEM((KEYS, TOK), F32),
            pltpu.VMEM((RATIO, TILES, TILE, QUARTER), F32),
            pltpu.VMEM((RATIO, TILES, TILE, QUARTER), F32),
            pltpu.VMEM((RATIO, TILES, 1, QUARTER), F32),
            pltpu.VMEM((RATIO, TILES, 1, QUARTER), F32),
            pltpu.VMEM((RATIO, TILES, 1, QUARTER), F32),
            pltpu.VMEM((RATIO, 1, QUARTER), F32),
            pltpu.VMEM((QUARTER, HEAD_DIM), F32),
            pltpu.VMEM((QUARTER, HEAD_DIM), F32),
            pltpu.VMEM((RATIO, QUARTER, HEAD_DIM), BF16),
            pltpu.VMEM((BACK, 2, QUARTER, HEAD_DIM), BF16),
            pltpu.VMEM((BACK, 2, QUARTER, HEAD_DIM), BF16),
            pltpu.VMEM((2, QUARTER, HEAD_DIM), BF16),
            dma((17,)),
            dma((13,)),
            dma((4 * SIDE,)),
            dma((5 * SIDE,)),
            dma((5,)),
        ],
        compiler_params=pltpu.CompilerParams(
            collective_id=0, has_side_effects=True, vmem_limit_bytes=60 * 1024 * 1024
        ),
    )(queries, grad_out, keys, values, doc_ids.reshape(1, TOK))
    return copied(outs)


def solution(mesh):
    return jax.shard_map(
        functools.partial(body, mesh.shape["grp"]),
        mesh=mesh,
        in_specs=(
            P(("grp", "sp"), None),
            P(("grp", "sp"), None),
            P(("grp", "sp"), None),
            P(("grp", "sp"), None),
            P(("grp", "sp")),
        ),
        out_specs=(P(("grp", "sp"), None), P(("grp", "sp"), None), P(("grp", "sp"), None)),
        check_vma=False,
    )
```
